32 devices in a mesh: row: 4 (over y, x), col: 8 (over z, core).
Axes of the slice: x: 2, y: 2, z: 4, core: 2. Of those that a mesh axis runs over, the one named last changes fastest.
Arguments:
- slab: bfloat16 [256, 128, 128], P(('row', 'col')), may hold values from -6 to 6
- pair: bfloat16 [256, 256, 128], P('row', 'col'), may hold values from -6 to 6
- mask: int32 [256], replicated, may hold values 0 or 1
- ln_gain: float32 [128], replicated, may hold values from 0.1 to 1.9
- w_query: bfloat16 [128, 128], replicated, may hold values from -0.5 to 0.5
- w_key: bfloat16 [128, 128], replicated, may hold values from -0.5 to 0.5
- w_value: bfloat16 [128, 128], replicated, may hold values from -0.5 to 0.5
- w_gate: bfloat16 [128, 128], replicated, may hold values from -0.5 to 0.5
- gate_bias: float32 [128], replicated, may hold values from -4 to 4
- w_bias: bfloat16 [128, 4], replicated, may hold values from -24 to 24
- w_out: bfloat16 [128, 128], replicated, may hold values from -0.5 to 0.5
- out_bias: float32 [128], replicated, may hold values from -3 to 3
Outputs:
- update: bfloat16 [256, 128, 128], P(('row', 'col'))
The draws below stay inside these ranges and needn't reach their ends.
Inputs may be any that keep to these rules, and one draw needn't show every extreme that they name: `mask`: 1 marks a real token, 0 a padding token.
All inputs are finite; a program needn't handle non-finite values.
Results may differ from the reference program's by a relative error of at most 0.01.
The reference program's roundings to bfloat16 on the way (of `tri_bias`, `weights` and `hidden`) count: a program that leaves them out, or rounds other values in their place, can miss the bound.
Values may be sent and summed in bfloat16 or wider, within the bound.
A program may use at most 128 MiB of HBM per device.

```python
import math
import jax
import jax.numpy as jnp
from jax import lax

TOK_BLK = 8
SLAB = 128
C = 128
H = 4
DH = 32
N = 256
N_ROW = 4
N_COL = 8


def draw_w_bias(key, part):
    raw = jax.random.normal(key, (C, H), jnp.float32)
    values = jnp.clip(raw / math.sqrt(C), -24.0, 24.0)
    return values.astype(jnp.bfloat16)


def place_ends(array, rng, low, high):
    place = [jax.random.randint(jax.random.fold_in(rng, axis), (), 0, length) for axis, length in enumerate(array.shape)]
    main_axis = array.shape.index(max(array.shape))
    neighbour = place[:main_axis] + [(place[main_axis] + 1) % array.shape[main_axis]] + place[main_axis + 1:]
    return array.at[tuple(place)].set(low).at[tuple(neighbour)].set(high)


def levels(own_key, extent, split, least, high):
    level = 1.0
    for position, blocks in split:
        steps = jax.random.uniform(jax.random.fold_in(jax.random.fold_in(own_key, 6), position), (blocks,), jnp.float32, least / len(split), high / len(split))
        level = level * jnp.repeat(jnp.exp(steps), extent[position] // blocks).reshape((-1,) + (1,) * (len(extent) - 1 - position))
    return level


def scatter_about(stream_key, extent, deviation, reach, pieces=(), kind=jnp.bfloat16):
    level = levels(stream_key, extent, pieces, -0.22, 0.18) if pieces else 1.0
    drawn = jax.random.normal(stream_key, extent, jnp.float32) * deviation * level
    return jnp.minimum(jnp.maximum(drawn, -reach), reach).astype(kind)


def setup_inputs(seed: int = 0) -> dict:
    streams_of = jax.random.split(jax.random.key(seed), 13)
    slab = scatter_about(streams_of[0], (N, SLAB, C), 1.0, 6.0, ((0, 32),))
    pair = scatter_about(streams_of[1], (N, N, C), 1.0, 6.0, ((0, 4), (1, 8)))
    mask = place_ends((jax.random.randint(streams_of[2], (N,), 0, 4) < 3).astype(jnp.int32), jax.random.fold_in(streams_of[2], 1), 0, 1)
    ln_gain = jnp.clip(1.0 + 0.18 * jax.random.normal(streams_of[3], (C,), jnp.float32), 0.1, 1.9)
    w_query = scatter_about(streams_of[4], (C, C), C ** -0.5, 0.5)
    w_key = scatter_about(streams_of[5], (C, C), C ** -0.5, 0.5)
    w_value = scatter_about(streams_of[6], (C, C), C ** -0.5, 0.5)
    w_gate = scatter_about(streams_of[7], (C, C), C ** -0.5, 0.5)
    gate_bias = scatter_about(streams_of[8], (C,), 1.0, 4.0, (), jnp.float32)
    w_bias = draw_w_bias(jax.random.fold_in(streams_of[12], 71), 0)
    w_out = scatter_about(streams_of[10], (C, C), C ** -0.5, 0.5)
    out_bias = scatter_about(streams_of[11], (C,), 0.5, 3.0, (), jnp.float32)
    return dict(slab=slab, pair=pair, mask=mask, ln_gain=ln_gain, w_query=w_query, w_key=w_key, w_value=w_value, w_gate=w_gate, gate_bias=gate_bias, w_bias=w_bias, w_out=w_out, out_bias=out_bias)


def normalize(values, ln_gain):
    values = values.astype(jnp.float32)
    center = lax.optimization_barrier(jnp.mean(values, axis=-1, keepdims=True))
    spread = lax.optimization_barrier(jnp.mean(jnp.square(values - center), axis=-1, keepdims=True))
    return ((values - center) * lax.rsqrt(spread + 1e-05) * ln_gain.astype(jnp.float32)).astype(jnp.bfloat16)

def project(rows, weight):
    flat = rows.reshape(-1, rows.shape[-1])
    result = jnp.dot(flat, weight, preferred_element_type=jnp.float32)
    return result.reshape(rows.shape[:-1] + (weight.shape[1],))

def reference(slab, pair, mask, ln_gain, w_query, w_key, w_value, w_gate, gate_bias, w_bias, w_out, out_bias):
    row_block = math.gcd(N, 32)

    def bias_rows(rows):
        return project(normalize(rows, ln_gain), w_bias).astype(jnp.bfloat16)
    tri_bias = lax.map(bias_rows, pair.reshape(N // row_block, row_block, N, C)).reshape(N, N, H)
    bias_heads = jnp.transpose(tri_bias, (2, 1, 0))
    normed_slab = normalize(slab, ln_gain)
    query = project(normed_slab, w_query).astype(jnp.bfloat16).reshape(N, SLAB, H, DH)
    key = project(normed_slab, w_key).astype(jnp.bfloat16).reshape(N, SLAB, H, DH)
    value = project(normed_slab, w_value).astype(jnp.bfloat16).reshape(N, SLAB, H, DH)
    gate = jax.nn.sigmoid(project(normed_slab, w_gate) + gate_bias)
    key_shift = (mask.astype(jnp.float32) - 1.0) * 1000000000.0
    scale = 1.0 / math.sqrt(DH)

    def column(inputs):
        query_col, key_col, value_col = inputs
        scores = jnp.einsum('ihd,khd->hik', query_col.astype(jnp.float32), key_col.astype(jnp.float32)) * scale
        scores = scores + bias_heads.astype(jnp.float32) + key_shift[None, None, :]
        top = lax.optimization_barrier(jnp.max(scores, axis=-1, keepdims=True))
        weights = jnp.exp(scores - top)
        grouped = weights.reshape(H, N, N_ROW, N_COL, TOK_BLK)
        rounded = grouped.astype(jnp.bfloat16).astype(jnp.float32)
        value_grouped = value_col.reshape(N_ROW, N_COL, TOK_BLK, H, DH).astype(jnp.float32)
        numer_parts = jnp.einsum('hiact,acthd->cihd', rounded, value_grouped)
        denom_parts = lax.optimization_barrier(jnp.sum(grouped, axis=(2, 4)))
        numer = lax.optimization_barrier(jnp.sum(numer_parts.astype(jnp.bfloat16).astype(jnp.float32), axis=0))
        denom = lax.optimization_barrier(jnp.sum(denom_parts.astype(jnp.bfloat16).astype(jnp.float32), axis=2))
        attended = numer / jnp.transpose(denom, (1, 0))[:, :, None]
        return attended.reshape(N, C)
    columns = (jnp.transpose(query, (1, 0, 2, 3)), jnp.transpose(key, (1, 0, 2, 3)), jnp.transpose(value, (1, 0, 2, 3)))
    attended = jnp.transpose(lax.map(column, columns), (1, 0, 2))
    hidden = (gate * attended).astype(jnp.bfloat16)
    update = project(hidden, w_out) + out_bias
    return update.astype(jnp.bfloat16)
```

```python
import functools
import math

import jax
import jax.numpy as jnp
from jax import lax
from jax.experimental import pallas as pl
from jax.experimental.pallas import tpu as pltpu
from jax.sharding import PartitionSpec as P

MESH = pl.DeviceIdType.MESH
F32 = jnp.float32
BF16 = jnp.bfloat16
NT = (((1,), (1,)), ((), ()))


def normalize(values, gain):
    center = jnp.mean(values, axis=-1, keepdims=True)
    moved = values - center
    spread = jnp.mean(jnp.square(moved), axis=-1, keepdims=True)
    return moved * lax.rsqrt(spread + 1e-05) * gain


def kernel(
    rows_count,
    cols_count,
    slab_ref,
    pair_ref,
    mask_ref,
    gain_ref,
    wq_ref,
    wk_ref,
    wv_ref,
    wg_ref,
    gate_bias_ref,
    wb_ref,
    wo_ref,
    out_bias_ref,
    out_ref,
    slab_f32,
    pair_f32,
    slab_send,
    slab_recv,
    bias,
    chunk_f32,
    query,
    key,
    value_t,
    gate,
    shift,
    back_send,
    back_recv,
    slab_ss,
    slab_rs,
    bias_ss,
    bias_rs,
    relay_ss,
    back_ss,
    back_rs,
):
    devices = rows_count * cols_count
    tok, width, channels = slab_ref.shape
    key_blk, query_blk, _ = pair_ref.shape
    heads = wb_ref.shape[1]
    head_dim = channels // heads
    cols = width // devices
    tokens = devices * tok
    lanes = heads * query_blk
    owners = query_blk // tok
    scale = 1.0 / math.sqrt(head_dim)
    my_row, my_col = lax.axis_index("row"), lax.axis_index("col")
    me = my_row * cols_count + my_col
    sibling = me + 1 - 2 * lax.rem(my_col, 2)
    cores = 2

    def place(p):
        return (p // cols_count, lax.rem(p, cols_count))

    barrier = pltpu.get_barrier_semaphore()

    def greet(n, carry):
        p = lax.rem(me + n, devices)
        pl.semaphore_signal(barrier, inc=1, device_id=place(p), device_id_type=MESH)
        return carry

    lax.fori_loop(1, devices, greet, 0)
    gain = gain_ref[...]
    for t in range(tok):
        slab_f32[t * width : (t + 1) * width, :] = normalize(slab_ref[t].astype(F32), gain)

    def chunk(p):
        parts = [
            slab_f32[pl.ds(p * cols + jj, tok, stride=width), :] for jj in range(cols)
        ]
        return jnp.concatenate(parts, axis=0).astype(BF16)

    slab_recv[me] = chunk(me)
    pl.semaphore_wait(barrier, devices - 1)

    def slab_copy(p):
        return pltpu.make_async_remote_copy(
            src_ref=slab_send.at[p],
            dst_ref=slab_recv.at[me],
            send_sem=slab_ss.at[p],
            recv_sem=slab_rs.at[me],
            device_id=place(p),
            device_id_type=MESH,
        )

    def send_slab(n, carry):
        p = lax.rem(me + n, devices)
        slab_send[p] = chunk(p)
        slab_copy(p).start()
        return carry

    lax.fori_loop(1, devices, send_slab, 0)

    pair_f32[...] = pair_ref[...].astype(F32).reshape(key_blk * query_blk, channels)
    lane_head = lax.broadcasted_iota(jnp.int32, (heads, lanes), 1) // query_blk
    spread_mat = (lane_head == lax.broadcasted_iota(jnp.int32, (heads, lanes), 0)).astype(F32)
    wide = jnp.dot(wb_ref[...], spread_mat.astype(BF16), preferred_element_type=F32)
    lane_query = lax.rem(lax.broadcasted_iota(jnp.int32, (channels, lanes), 1), query_blk)

    def bias_step(il, total):
        rows = pair_f32[pl.ds(il, key_blk, stride=query_blk), :]
        normed = normalize(rows, gain).astype(BF16)
        weight = jnp.where(lane_query == il, wide, 0.0).astype(BF16)
        return total + jnp.dot(normed, weight, preferred_element_type=F32)

    total = lax.fori_loop(
        0, query_blk, bias_step, jnp.zeros((key_blk, lanes), F32), unroll=8
    )
    bias[my_col, my_row] = total.astype(BF16)

    def bias_copy(p):
        return pltpu.make_async_remote_copy(
            src_ref=bias.at[my_col, my_row],
            dst_ref=bias.at[my_col, my_row],
            send_sem=bias_ss.at[p],
            recv_sem=bias_rs.at[me],
            device_id=place(p),
            device_id_type=MESH,
        )

    def relay_copy(s):
        r, c = place(s)
        return pltpu.make_async_remote_copy(
            src_ref=bias.at[c, r],
            dst_ref=bias.at[c, r],
            send_sem=relay_ss.at[s],
            recv_sem=bias_rs.at[s],
            device_id=place(sibling),
            device_id_type=MESH,
        )

    def bias_wait(s):
        r, c = place(s)
        pltpu.make_async_remote_copy(
            src_ref=bias.at[c, r],
            dst_ref=bias.at[c, r],
            send_sem=relay_ss.at[s],
            recv_sem=bias_rs.at[s],
            device_id=place(sibling),
            device_id_type=MESH,
        ).wait_recv()

    bias_copy(sibling).start()

    def send_bias(n, carry):
        bias_copy(lax.rem(me + cores * n, devices)).start()
        return carry

    lax.fori_loop(1, devices // cores, send_bias, 0)

    def take_slab(n, carry):
        s = lax.rem(me + devices - n, devices)
        pltpu.make_async_remote_copy(
            src_ref=slab_send.at[s],
            dst_ref=slab_recv.at[s],
            send_sem=slab_ss.at[s],
            recv_sem=slab_rs.at[s],
            device_id=place(s),
            device_id_type=MESH,
        ).wait_recv()
        return carry

    lax.fori_loop(1, devices, take_slab, 0)
    chunk_f32[...] = slab_recv[...].astype(F32)
    value_w = wv_ref[...].astype(F32).T.astype(BF16)
    for jj in range(cols):
        rows = chunk_f32[:, jj * tok : (jj + 1) * tok, :].reshape(tokens, channels).astype(BF16)
        query[jj] = jnp.dot(rows, wq_ref[...], preferred_element_type=F32).astype(BF16)
        key[jj] = jnp.dot(rows, wk_ref[...], preferred_element_type=F32).astype(BF16)
        value_t[jj] = lax.dot_general(
            value_w, rows, NT, preferred_element_type=F32
        ).astype(BF16)
        gate[jj] = jax.nn.sigmoid(
            jnp.dot(rows, wg_ref[...], preferred_element_type=F32) + gate_bias_ref[...]
        )
    shift_row = (mask_ref[...].astype(F32) - 1.0) * 1000000000.0
    shift[...] = jnp.broadcast_to(shift_row, (lanes, tokens)).T

    def relay(n, carry):
        s = lax.rem(me + devices - cores * n, devices)
        bias_wait(s)
        relay_copy(s).start()
        return carry

    lax.fori_loop(1, devices // cores, relay, 0)

    row_head = lax.broadcasted_iota(jnp.int32, (lanes, channels), 0) // query_blk
    chan_head = lax.broadcasted_iota(jnp.int32, (lanes, channels), 1) // head_dim
    own_head = row_head == chan_head

    def back_copy(p):
        return pltpu.make_async_remote_copy(
            src_ref=back_send.at[p],
            dst_ref=back_recv.at[me],
            send_sem=back_ss.at[p],
            recv_sem=back_rs.at[me],
            device_id=place(p),
            device_id_type=MESH,
        )

    def attend(n, carry):
        c = lax.rem(my_col + n, cols_count)
        for r in range(rows_count):
            s = r * cols_count + c

            @pl.when(lax.rem(c + my_col, 2) == 1)
            def _():
                bias_wait(s)

        bias_f32 = bias[c].astype(F32).reshape(tokens, lanes)
        at = pl.multiple_of(c * query_blk, query_blk)
        hidden = []
        for jj in range(cols):
            q_rows = query[jj, pl.ds(at, query_blk), :].astype(F32)
            q_heads = jnp.where(
                own_head, jnp.concatenate([q_rows] * heads, axis=0), 0.0
            ).astype(BF16)
            scores = lax.dot_general(key[jj], q_heads, NT, preferred_element_type=F32) * scale
            scores = (scores + bias_f32) + shift[...]
            top = jnp.max(scores, axis=0, keepdims=True)
            weights = jnp.exp(scores - top)
            denom = jnp.sum(weights, axis=0, keepdims=True)
            numer = jnp.dot(value_t[jj], weights.astype(BF16), preferred_element_type=F32)
            spread = jnp.where(own_head, (numer * (1.0 / denom)).T, 0.0)
            attended = spread[:query_blk]
            for h in range(1, heads):
                attended = attended + spread[h * query_blk : (h + 1) * query_blk]
            hidden.append((gate[jj, pl.ds(at, query_blk), :] * attended).astype(BF16))
        update = (
            jnp.dot(jnp.concatenate(hidden, axis=0), wo_ref[...], preferred_element_type=F32)
            + out_bias_ref[...]
        )
        for o in range(owners):
            p = c * owners + o
            part = jnp.concatenate(
                [
                    update[jj * query_blk + o * tok : jj * query_blk + (o + 1) * tok]
                    for jj in range(cols)
                ],
                axis=0,
            ).astype(BF16)

            @pl.when(p == me)
            def _():
                back_recv[me] = part

            @pl.when(p != me)
            def _():
                back_send[p] = part
                back_copy(p).start()

        return carry

    lax.fori_loop(0, cols_count, attend, 0)

    def take_back(n, carry):
        s = lax.rem(me + devices - n, devices)
        pltpu.make_async_remote_copy(
            src_ref=back_send.at[s],
            dst_ref=back_recv.at[s],
            send_sem=back_ss.at[s],
            recv_sem=back_rs.at[s],
            device_id=place(s),
            device_id_type=MESH,
        ).wait_recv()
        return carry

    lax.fori_loop(1, devices, take_back, 0)
    slab_f32[...] = back_recv[...].astype(F32).reshape(width * tok, channels)
    for t in range(tok):
        out_ref[t] = slab_f32[pl.ds(t, width, stride=tok), :].astype(BF16)

    def drain(n, carry):
        p = lax.rem(me + n, devices)
        slab_copy(p).wait_send()
        back_copy(p).wait_send()
        return carry

    lax.fori_loop(1, devices, drain, 0)
    bias_copy(sibling).wait_send()

    def drain_bias(n, carry):
        bias_copy(lax.rem(me + cores * n, devices)).wait_send()
        relay_copy(lax.rem(me + devices - cores * n, devices)).wait_send()
        return carry

    lax.fori_loop(1, devices // cores, drain_bias, 0)


def per_device(
    slab, pair, mask, ln_gain, w_query, w_key, w_value, w_gate, gate_bias, w_bias, w_out, out_bias
):
    rows_count = lax.axis_size("row")
    cols_count = lax.axis_size("col")
    devices = rows_count * cols_count
    tok, width, channels = slab.shape
    key_blk, query_blk, _ = pair.shape
    heads = w_bias.shape[1]
    cols = width // devices
    tokens = devices * tok
    lanes = heads * query_blk
    dma = pltpu.SemaphoreType.DMA((devices,))
    vmem = pltpu.VMEM
    return pl.pallas_call(
        functools.partial(kernel, rows_count, cols_count),
        out_shape=jax.ShapeDtypeStruct(slab.shape, BF16),
        in_specs=[pl.BlockSpec(memory_space=vmem)] * 12,
        out_specs=pl.BlockSpec(memory_space=vmem),
        scratch_shapes=[
            vmem((tok * width, channels), F32),
            vmem((key_blk * query_blk, channels), F32),
            vmem((devices, cols * tok, channels), BF16),
            vmem((devices, cols * tok, channels), BF16),
            vmem((cols_count, rows_count, key_blk, lanes), BF16),
            vmem((devices, cols * tok, channels), F32),
            vmem((cols, tokens, channels), BF16),
            vmem((cols, tokens, channels), BF16),
            vmem((cols, channels, tokens), BF16),
            vmem((cols, tokens, channels), F32),
            vmem((tokens, lanes), F32),
            vmem((devices, cols * tok, channels), BF16),
            vmem((devices, cols * tok, channels), BF16),
            dma,
            dma,
            dma,
            dma,
            dma,
            dma,
            dma,
        ],
        compiler_params=pltpu.CompilerParams(
            collective_id=0, has_side_effects=True, vmem_limit_bytes=48 * 1024 * 1024
        ),
        cost_estimate=pl.CostEstimate(
            flops=2 * tokens * tokens * heads * channels * cols * 2,
            bytes_accessed=4 * slab.size,
            transcendentals=tokens * tokens * heads * cols,
        ),
        name="triangle",
    )(
        slab,
        pair,
        mask.reshape(1, -1),
        ln_gain.reshape(1, -1),
        w_query,
        w_key,
        w_value,
        w_gate,
        gate_bias.reshape(1, -1),
        w_bias,
        w_out,
        out_bias.reshape(1, -1),
    )


def solution(mesh):
    placed = (P(("row", "col"), None, None), P("row", "col", None)) + (P(),) * 10
    return jax.shard_map(
        per_device,
        mesh=mesh,
        in_specs=placed,
        out_specs=P(("row", "col"), None, None),
        check_vma=False,
    )
```

```python
import functools
import math

import jax
import jax.numpy as jnp
from jax import lax
from jax.experimental import pallas as pl
from jax.experimental.pallas import tpu as pltpu
from jax.sharding import PartitionSpec as P

MESH = pl.DeviceIdType.MESH
F32 = jnp.float32
BF16 = jnp.bfloat16
NT = (((1,), (1,)), ((), ()))


def normalize(values, gain):
    center = jnp.mean(values, axis=-1, keepdims=True)
    moved = values - center
    spread = jnp.mean(jnp.square(moved), axis=-1, keepdims=True)
    return moved * lax.rsqrt(spread + 1e-05) * gain


def kernel(rows_count, cols_count, *refs):
    hbm, out_ref = refs[:12], refs[12]
    (
        slab_ref,
        pair_ref,
        mask_ref,
        gain_ref,
        wq_ref,
        wk_ref,
        wv_ref,
        wg_ref,
        gate_bias_ref,
        wb_ref,
        wo_ref,
        out_bias_ref,
    ) = local = refs[13:25]
    (
        slab_f32,
        pair_f32,
        slab_send,
        slab_recv,
        bias,
        chunk_f32,
        query,
        key,
        value_t,
        gate,
        shift,
        back_send,
        back_recv,
        in_sem,
        slab_ss,
        slab_rs,
        line_ss,
        line_rs,
        plane_ss,
        plane_rs,
        core_ss,
        core_rs,
        back_ss,
        back_rs,
    ) = refs[25:]
    devices = rows_count * cols_count
    tok, width, channels = slab_ref.shape
    key_blk, query_blk, _ = pair_ref.shape
    heads = wb_ref.shape[0]
    head_dim = channels // heads
    cols = width // devices
    tokens = devices * tok
    lanes = heads * query_blk
    owners = query_blk // tok
    scale = 1.0 / math.sqrt(head_dim)
    cores = 2
    line = cols_count // cores
    my_row, my_col = lax.axis_index("row"), lax.axis_index("col")
    my_line, core = lax.div(my_col, cores), lax.rem(my_col, cores)
    me = my_row * cols_count + my_col

    def fetch(i):
        return pltpu.make_async_copy(hbm[i], local[i], in_sem.at[i])

    for i in (0, 3, 1, 9, 2, 4, 5, 6, 7, 8, 10, 11):
        fetch(i).start()

    def place(p):
        return (lax.div(p, cols_count), lax.rem(p, cols_count))

    def wait_bytes(ref, sem):
        pltpu.make_async_copy(ref, ref, sem).wait()

    def send(src, dst, send_sem, recv_sem, target):
        pltpu.make_async_remote_copy(
            src_ref=src,
            dst_ref=dst,
            send_sem=send_sem,
            recv_sem=recv_sem,
            device_id=target,
            device_id_type=MESH,
        ).start()

    barrier = pltpu.get_barrier_semaphore()

    def greet(n, carry):
        p = lax.rem(me + n, devices)
        pl.semaphore_signal(barrier, inc=1, device_id=place(p), device_id_type=MESH)
        return carry

    lax.fori_loop(1, devices, greet, 0)

    fetch(0).wait()
    fetch(3).wait()
    gain = gain_ref[...]
    for t in range(tok):
        slab_f32[t * width : (t + 1) * width, :] = normalize(slab_ref[t].astype(F32), gain)
    for p in range(devices):
        parts = [
            slab_f32[pl.ds(p * cols + jj, tok, stride=width), :] for jj in range(cols)
        ]
        slab_send[p] = jnp.concatenate(parts, axis=0).astype(BF16)
    slab_recv[me] = slab_send[me]
    pl.semaphore_wait(barrier, devices - 1)

    def send_slab(n, carry):
        p = lax.rem(me + n, devices)
        send(slab_send.at[p], slab_recv.at[me], slab_ss, slab_rs, place(p))
        return carry

    lax.fori_loop(1, devices, send_slab, 0)

    fetch(1).wait()
    fetch(9).wait()
    pair_f32[...] = pair_ref[...].astype(F32).reshape(key_blk * query_blk, channels)
    lane_head = lax.broadcasted_iota(jnp.int32, (heads, lanes), 1) // query_blk
    spread_mat = (lane_head == lax.broadcasted_iota(jnp.int32, (heads, lanes), 0)).astype(F32)
    wide = lax.dot_general(
        wb_ref[...],
        spread_mat.astype(BF16),
        (((0,), (0,)), ((), ())),
        preferred_element_type=F32,
    )
    lane_query = lax.rem(lax.broadcasted_iota(jnp.int32, (channels, lanes), 1), query_blk)

    def bias_step(il, total):
        rows = pair_f32[pl.ds(il, key_blk, stride=query_blk), :]
        normed = normalize(rows, gain).astype(BF16)
        weight = jnp.where(lane_query == il, wide, 0.0).astype(BF16)
        return total + jnp.dot(normed, weight, preferred_element_type=F32)

    total = lax.fori_loop(
        0, query_blk, bias_step, jnp.zeros((key_blk, lanes), F32), unroll=8
    )
    bias[core, my_row, my_line] = total.astype(BF16)
    for n in range(1, line):
        z = lax.rem(my_line + n, line)
        tile = bias.at[core, my_row, my_line]
        send(tile, tile, line_ss, line_rs, (my_row, z * cores + core))

    wait_bytes(slab_recv.at[pl.ds(0, devices - 1)], slab_rs)
    chunk_f32[...] = slab_recv[...].astype(F32)

    wait_bytes(bias.at[core, my_row, pl.ds(0, line - 1)], line_rs)
    block = bias.at[core, my_row]
    for n in range(1, rows_count):
        r = lax.rem(my_row + n, rows_count)
        send(block, block, plane_ss, plane_rs, (r, my_col))
    send(block, block, core_ss, core_rs, (my_row, my_col + 1 - 2 * core))

    for i in (2, 4, 5, 6, 7, 8, 10, 11):
        fetch(i).wait()
    value_w = wv_ref[...].astype(F32).T.astype(BF16)
    for jj in range(cols):
        rows = chunk_f32[:, jj * tok : (jj + 1) * tok, :].reshape(tokens, channels).astype(BF16)
        query[jj] = jnp.dot(rows, wq_ref[...], preferred_element_type=F32).astype(BF16)
        key[jj] = jnp.dot(rows, wk_ref[...], preferred_element_type=F32).astype(BF16)
        value_t[jj] = lax.dot_general(
            value_w, rows, NT, preferred_element_type=F32
        ).astype(BF16)
        gate[jj] = jax.nn.sigmoid(
            jnp.dot(rows, wg_ref[...], preferred_element_type=F32) + gate_bias_ref[...]
        )
    shift_row = (mask_ref[...].astype(F32) - 1.0) * 1000000000.0
    shift[...] = jnp.broadcast_to(shift_row, (lanes, tokens)).T

    wait_bytes(bias.at[core, pl.ds(0, rows_count - 1)], plane_rs)
    for n in range(1, rows_count):
        other = bias.at[core, lax.rem(my_row + n, rows_count)]
        send(other, other, core_ss, core_rs, (my_row, my_col + 1 - 2 * core))

    row_head = lax.broadcasted_iota(jnp.int32, (lanes, channels), 0) // query_blk
    chan_head = lax.broadcasted_iota(jnp.int32, (lanes, channels), 1) // head_dim
    own_head = row_head == chan_head

    def attend_block(half, z):
        c = z * cores + half
        bias_f32 = bias[half, :, z].astype(F32).reshape(tokens, lanes)
        at = pl.multiple_of(c * query_blk, query_blk)
        hidden = []
        for jj in range(cols):
            q_rows = query[jj, pl.ds(at, query_blk), :].astype(F32)
            q_heads = jnp.where(
                own_head, jnp.concatenate([q_rows] * heads, axis=0), 0.0
            ).astype(BF16)
            scores = lax.dot_general(key[jj], q_heads, NT, preferred_element_type=F32) * scale
            scores = (scores + bias_f32) + shift[...]
            top = jnp.max(scores, axis=0, keepdims=True)
            weights = jnp.exp(scores - top)
            denom = jnp.sum(weights, axis=0, keepdims=True)
            numer = jnp.dot(value_t[jj], weights.astype(BF16), preferred_element_type=F32)
            spread = jnp.where(own_head, (numer * (1.0 / denom)).T, 0.0)
            attended = spread[:query_blk]
            for h in range(1, heads):
                attended = attended + spread[h * query_blk : (h + 1) * query_blk]
            hidden.append((gate[jj, pl.ds(at, query_blk), :] * attended).astype(BF16))
        update = (
            jnp.dot(jnp.concatenate(hidden, axis=0), wo_ref[...], preferred_element_type=F32)
            + out_bias_ref[...]
        )
        for o in range(owners):
            back_send[c * owners + o] = jnp.concatenate(
                [
                    update[jj * query_blk + o * tok : jj * query_blk + (o + 1) * tok]
                    for jj in range(cols)
                ],
                axis=0,
            ).astype(BF16)

    def send_back(half, z):
        for o in range(owners):
            p = (z * cores + half) * owners + o

            @pl.when(p != me)
            def _():
                send(back_send.at[p], back_recv.at[me], back_ss, back_rs, place(p))

    pair_step = 2 if line % 2 == 0 else 1

    def attend_half(half):
        def step(n, carry):
            first = lax.rem(lax.div(my_line, pair_step) + n, line // pair_step) * pair_step
            for m in range(pair_step):
                attend_block(half, first + m)
            for m in range(pair_step):
                send_back(half, first + m)
            return carry

        lax.fori_loop(0, line // pair_step, step, 0)

    attend_half(core)
    wait_bytes(bias.at[1 - core], core_rs)
    attend_half(1 - core)
    back_recv[me] = back_send[me]

    wait_bytes(slab_send.at[pl.ds(0, devices - 1)], slab_ss)
    wait_bytes(bias.at[core, my_row, pl.ds(0, line - 1)], line_ss)
    wait_bytes(bias.at[core, pl.ds(0, rows_count - 1)], plane_ss)
    wait_bytes(bias.at[core], core_ss)
    wait_bytes(back_send.at[pl.ds(0, devices - 1)], back_ss)

    wait_bytes(back_recv.at[pl.ds(0, devices - 1)], back_rs)
    slab_f32[...] = back_recv[...].astype(F32).reshape(width * tok, channels)
    for t in range(tok):
        out_ref[t] = slab_f32[pl.ds(t, width, stride=tok), :].astype(BF16)


def per_device(
    slab, pair, mask, ln_gain, w_query, w_key, w_value, w_gate, gate_bias, w_bias, w_out, out_bias
):
    rows_count = lax.axis_size("row")
    cols_count = lax.axis_size("col")
    devices = rows_count * cols_count
    tok, width, channels = slab.shape
    key_blk, query_blk, _ = pair.shape
    heads = w_bias.shape[1]
    cols = width // devices
    tokens = devices * tok
    lanes = heads * query_blk
    operands = (
        slab,
        pair,
        mask.reshape(1, -1),
        ln_gain.reshape(1, -1),
        w_query,
        w_key,
        w_value,
        w_gate,
        gate_bias.reshape(1, -1),
        w_bias.T,
        w_out,
        out_bias.reshape(1, -1),
    )
    dma = pltpu.SemaphoreType.DMA
    vmem = pltpu.VMEM
    return pl.pallas_call(
        functools.partial(kernel, rows_count, cols_count),
        out_shape=jax.ShapeDtypeStruct(slab.shape, BF16),
        in_specs=[pl.BlockSpec(memory_space=pltpu.HBM)] * len(operands),
        out_specs=pl.BlockSpec(memory_space=vmem),
        scratch_shapes=[vmem(x.shape, x.dtype) for x in operands]
        + [
            vmem((tok * width, channels), F32),
            vmem((key_blk * query_blk, channels), F32),
            vmem((devices, cols * tok, channels), BF16),
            vmem((devices, cols * tok, channels), BF16),
            vmem((2, rows_count, cols_count // 2, key_blk, lanes), BF16),
            vmem((devices, cols * tok, channels), F32),
            vmem((cols, tokens, channels), BF16),
            vmem((cols, tokens, channels), BF16),
            vmem((cols, channels, tokens), BF16),
            vmem((cols, tokens, channels), F32),
            vmem((tokens, lanes), F32),
            vmem((devices, cols * tok, channels), BF16),
            vmem((devices, cols * tok, channels), BF16),
            dma((len(operands),)),
        ]
        + [dma] * 10,
        compiler_params=pltpu.CompilerParams(
            collective_id=0, has_side_effects=True, vmem_limit_bytes=56 * 1024 * 1024
        ),
        cost_estimate=pl.CostEstimate(
            flops=2 * tokens * tokens * heads * channels * cols * 2,
            bytes_accessed=4 * slab.size,
            transcendentals=tokens * tokens * heads * cols,
        ),
        name="triangle",
    )(*operands)


def solution(mesh):
    placed = (P(("row", "col"), None, None), P("row", "col", None)) + (P(),) * 10
    return jax.shard_map(
        per_device,
        mesh=mesh,
        in_specs=placed,
        out_specs=P(("row", "col"), None, None),
        check_vma=False,
    )
```

```python
import functools
import math

import jax
import jax.numpy as jnp
from jax import lax
from jax.experimental import pallas as pl
from jax.experimental.pallas import tpu as pltpu
from jax.sharding import PartitionSpec as P

MESH = pl.DeviceIdType.MESH
F32 = jnp.float32
BF16 = jnp.bfloat16
NT = (((1,), (1,)), ((), ()))


def normalize(values, gain):
    center = jnp.mean(values, axis=-1, keepdims=True)
    moved = values - center
    spread = jnp.mean(jnp.square(moved), axis=-1, keepdims=True)
    return moved * lax.rsqrt(spread + 1e-05) * gain


def kernel(rows_count, cols_count, *refs):
    hbm, out_ref = refs[:12], refs[12]
    (
        slab_ref,
        pair_ref,
        mask_ref,
        gain_ref,
        wq_ref,
        wk_ref,
        wv_ref,
        wg_ref,
        gate_bias_ref,
        wb_ref,
        wo_ref,
        out_bias_ref,
    ) = local = refs[13:25]
    (
        slab_f32,
        slab_send,
        slab_recv,
        bias,
        chunk_f32,
        query,
        key,
        value_t,
        gate,
        shift,
        back_send,
        back_recv,
        in_sem,
        slab_ss,
        slab_rs,
        line_ss,
        line_rs,
        plane_ss,
        plane_rs,
        core_ss,
        core_rs,
        back_ss,
        back_rs,
    ) = refs[25:]
    devices = rows_count * cols_count
    tok, width, channels = slab_ref.shape
    key_blk, query_blk, _ = pair_ref.shape
    heads = wb_ref.shape[0]
    head_dim = channels // heads
    cols = width // devices
    tokens = devices * tok
    lanes = heads * query_blk
    owners = query_blk // tok
    scale = 1.0 / math.sqrt(head_dim)
    cores = 2
    line = cols_count // cores
    group = 2 - line % 2
    my_row, my_col = lax.axis_index("row"), lax.axis_index("col")
    my_line, core = lax.div(my_col, cores), lax.rem(my_col, cores)
    me = my_row * cols_count + my_col

    def fetch(i):
        return pltpu.make_async_copy(hbm[i], local[i], in_sem.at[i])

    for i in (0, 3, 1, 9, 2, 4, 5, 6, 7, 8, 10, 11):
        fetch(i).start()

    def place(p):
        return (lax.div(p, cols_count), lax.rem(p, cols_count))

    def wait_bytes(ref, sem):
        pltpu.make_async_copy(ref, ref, sem).wait()

    def send(src, dst, send_sem, recv_sem, target):
        pltpu.make_async_remote_copy(
            src_ref=src,
            dst_ref=dst,
            send_sem=send_sem,
            recv_sem=recv_sem,
            device_id=target,
            device_id_type=MESH,
        ).start()

    barrier = pltpu.get_barrier_semaphore()

    def greet(n, carry):
        p = lax.rem(me + n, devices)
        pl.semaphore_signal(barrier, inc=1, device_id=place(p), device_id_type=MESH)
        return carry

    lax.fori_loop(1, devices, greet, 0)

    fetch(0).wait()
    fetch(3).wait()
    gain = gain_ref[...]
    for t in range(tok):
        slab_f32[t * width : (t + 1) * width, :] = normalize(slab_ref[t].astype(F32), gain)
    for p in range(devices):
        parts = [
            slab_f32[pl.ds(p * cols + jj, tok, stride=width), :] for jj in range(cols)
        ]
        slab_send[p] = jnp.concatenate(parts, axis=0).astype(BF16)
    slab_recv[me] = slab_send[me]
    pl.semaphore_wait(barrier, devices - 1)

    def send_slab(n, carry):
        p = lax.rem(me + n, devices)
        send(slab_send.at[p], slab_recv.at[me], slab_ss, slab_rs, place(p))
        return carry

    lax.fori_loop(1, devices, send_slab, 0)

    fetch(1).wait()
    fetch(9).wait()
    lane_head = lax.broadcasted_iota(jnp.int32, (heads, lanes), 1) // query_blk
    spread_mat = (lane_head == lax.broadcasted_iota(jnp.int32, (heads, lanes), 0)).astype(F32)
    wide = lax.dot_general(
        wb_ref[...],
        spread_mat.astype(BF16),
        (((0,), (0,)), ((), ())),
        preferred_element_type=F32,
    ).astype(BF16)
    part = 16
    lane_query = lax.rem(lax.broadcasted_iota(jnp.int32, (part, query_blk, lanes), 2), query_blk)
    own_query = lane_query == lax.broadcasted_iota(jnp.int32, (part, query_blk, lanes), 1)
    for k in range(0, key_blk, part):
        rows = pair_ref[k : k + part].astype(F32).reshape(part * query_blk, channels)
        normed = normalize(rows, gain).astype(BF16)
        spread = jnp.dot(normed, wide, preferred_element_type=F32)
        spread = jnp.where(own_query, spread.reshape(part, query_blk, lanes), 0.0)
        bias[core, my_row, my_line, k : k + part, :] = jnp.sum(spread, axis=1).astype(BF16)
    for n in range(1, line):
        z = lax.rem(my_line + n, line)
        tile = bias.at[core, my_row, my_line]
        send(tile, tile, line_ss, line_rs, (my_row, z * cores + core))

    wait_bytes(slab_recv.at[pl.ds(0, devices - 1)], slab_rs)
    chunk_f32[...] = slab_recv[...].astype(F32)

    wait_bytes(bias.at[core, my_row, pl.ds(0, line - 1)], line_rs)
    block = bias.at[core, my_row]
    for n in range(1, rows_count):
        r = lax.rem(my_row + n, rows_count)
        send(block, block, plane_ss, plane_rs, (r, my_col))
    send(block, block, core_ss, core_rs, (my_row, my_col + 1 - 2 * core))

    for i in (2, 4, 5, 6, 7, 8, 10, 11):
        fetch(i).wait()
    weights_qkg = jnp.concatenate([wq_ref[...], wk_ref[...], wg_ref[...]], axis=1)
    value_w = wv_ref[...].astype(F32).T.astype(BF16)
    for jj in range(cols):
        rows = chunk_f32[:, jj * tok : (jj + 1) * tok, :].reshape(tokens, channels).astype(BF16)
        value_t[jj] = lax.dot_general(
            value_w, rows, NT, preferred_element_type=F32
        ).astype(BF16)
        joined = jnp.dot(rows, weights_qkg, preferred_element_type=F32)
        query[jj] = joined[:, :channels].astype(BF16)
        key[jj] = joined[:, channels : 2 * channels].astype(BF16)
        gate[jj] = jax.nn.sigmoid(joined[:, 2 * channels :] + gate_bias_ref[...])
    shift_row = (mask_ref[...].astype(F32) - 1.0) * 1000000000.0
    shift[...] = jnp.broadcast_to(shift_row, (group * lanes, tokens)).T

    wait_bytes(bias.at[core, pl.ds(0, rows_count - 1)], plane_rs)
    for n in range(1, rows_count):
        other = bias.at[core, lax.rem(my_row + n, rows_count)]
        send(other, other, core_ss, core_rs, (my_row, my_col + 1 - 2 * core))

    row_head = lax.broadcasted_iota(jnp.int32, (group * lanes, channels), 0) // query_blk
    chan_head = lax.broadcasted_iota(jnp.int32, (group * lanes, channels), 1) // head_dim
    own_head = lax.rem(row_head, heads) == chan_head

    def attend_blocks(half, z):
        bias_f32 = jnp.concatenate(
            [bias[half, :, z + m].astype(F32).reshape(tokens, lanes) for m in range(group)], axis=1
        )
        at = [
            pl.multiple_of(((z + m) * cores + half) * query_blk, query_blk) for m in range(group)
        ]
        hidden = []
        for jj in range(cols):
            copies = []
            for m in range(group):
                copies += [query[jj, pl.ds(at[m], query_blk), :].astype(F32)] * heads
            q_heads = jnp.where(own_head, jnp.concatenate(copies, axis=0), 0.0).astype(BF16)
            scores = lax.dot_general(key[jj], q_heads, NT, preferred_element_type=F32) * scale
            scores = (scores + bias_f32) + shift[...]
            top = jnp.max(scores, axis=0, keepdims=True)
            weights = jnp.exp(scores - top)
            denom = jnp.sum(weights, axis=0, keepdims=True)
            numer = jnp.dot(value_t[jj], weights.astype(BF16), preferred_element_type=F32)
            spread = jnp.where(own_head, (numer * (1.0 / denom)).T, 0.0)
            for m in range(group):
                base = m * lanes
                attended = spread[base : base + query_blk]
                for h in range(1, heads):
                    start = base + h * query_blk
                    attended = attended + spread[start : start + query_blk]
                hidden.append((gate[jj, pl.ds(at[m], query_blk), :] * attended).astype(BF16))
        update = (
            jnp.dot(jnp.concatenate(hidden, axis=0), wo_ref[...], preferred_element_type=F32)
            + out_bias_ref[...]
        )
        for m in range(group):
            for o in range(owners):
                starts = [(jj * group + m) * query_blk + o * tok for jj in range(cols)]
                back_send[((z + m) * cores + half) * owners + o] = jnp.concatenate(
                    [update[start : start + tok] for start in starts], axis=0
                ).astype(BF16)

    def send_back(half, z):
        for o in range(owners):
            p = (z * cores + half) * owners + o

            @pl.when(p != me)
            def _():
                send(back_send.at[p], back_recv.at[me], back_ss, back_rs, place(p))

    def attend_half(half):
        def step(n, carry):
            first = lax.rem(lax.div(my_line, group) + n, line // group) * group
            attend_blocks(half, first)
            for m in range(group):
                send_back(half, first + m)
            return carry

        lax.fori_loop(0, line // group, step, 0)

    attend_half(core)
    wait_bytes(bias.at[1 - core], core_rs)
    attend_half(1 - core)
    back_recv[me] = back_send[me]

    wait_bytes(slab_send.at[pl.ds(0, devices - 1)], slab_ss)
    wait_bytes(bias.at[core, my_row, pl.ds(0, line - 1)], line_ss)
    wait_bytes(bias.at[core, pl.ds(0, rows_count - 1)], plane_ss)
    wait_bytes(bias.at[core], core_ss)
    wait_bytes(back_send.at[pl.ds(0, devices - 1)], back_ss)

    wait_bytes(back_recv.at[pl.ds(0, devices - 1)], back_rs)
    slab_f32[...] = back_recv[...].astype(F32).reshape(width * tok, channels)
    for t in range(tok):
        out_ref[t] = slab_f32[pl.ds(t, width, stride=tok), :].astype(BF16)


def per_device(
    slab, pair, mask, ln_gain, w_query, w_key, w_value, w_gate, gate_bias, w_bias, w_out, out_bias
):
    rows_count = lax.axis_size("row")
    cols_count = lax.axis_size("col")
    devices = rows_count * cols_count
    tok, width, channels = slab.shape
    key_blk, query_blk, _ = pair.shape
    heads = w_bias.shape[1]
    cols = width // devices
    tokens = devices * tok
    lanes = heads * query_blk
    group = 2 - (cols_count // 2) % 2
    operands = (
        slab,
        pair,
        mask.reshape(1, -1),
        ln_gain.reshape(1, -1),
        w_query,
        w_key,
        w_value,
        w_gate,
        gate_bias.reshape(1, -1),
        w_bias.T,
        w_out,
        out_bias.reshape(1, -1),
    )
    dma = pltpu.SemaphoreType.DMA
    vmem = pltpu.VMEM
    return pl.pallas_call(
        functools.partial(kernel, rows_count, cols_count),
        out_shape=jax.ShapeDtypeStruct(slab.shape, BF16),
        in_specs=[pl.BlockSpec(memory_space=pltpu.HBM)] * len(operands),
        out_specs=pl.BlockSpec(memory_space=vmem),
        scratch_shapes=[vmem(x.shape, x.dtype) for x in operands]
        + [
            vmem((tok * width, channels), F32),
            vmem((devices, cols * tok, channels), BF16),
            vmem((devices, cols * tok, channels), BF16),
            vmem((2, rows_count, cols_count // 2, key_blk, lanes), BF16),
            vmem((devices, cols * tok, channels), F32),
            vmem((cols, tokens, channels), BF16),
            vmem((cols, tokens, channels), BF16),
            vmem((cols, channels, tokens), BF16),
            vmem((cols, tokens, channels), F32),
            vmem((tokens, group * lanes), F32),
            vmem((devices, cols * tok, channels), BF16),
            vmem((devices, cols * tok, channels), BF16),
            dma((len(operands),)),
        ]
        + [dma] * 10,
        compiler_params=pltpu.CompilerParams(
            collective_id=0, has_side_effects=True, vmem_limit_bytes=56 * 1024 * 1024
        ),
        cost_estimate=pl.CostEstimate(
            flops=2 * tokens * tokens * heads * channels * cols * 2,
            bytes_accessed=4 * slab.size,
            transcendentals=tokens * tokens * heads * cols,
        ),
        name="triangle",
    )(*operands)


def solution(mesh):
    placed = (P(("row", "col"), None, None), P("row", "col", None)) + (P(),) * 10
    return jax.shard_map(
        per_device,
        mesh=mesh,
        in_specs=placed,
        out_specs=P(("row", "col"), None, None),
        check_vma=False,
    )
```

```python
import functools
import math

import jax
import jax.numpy as jnp
from jax import lax
from jax.experimental import pallas as pl
from jax.experimental.pallas import tpu as pltpu
from jax.sharding import PartitionSpec as P

MESH = pl.DeviceIdType.MESH
F32 = jnp.float32
BF16 = jnp.bfloat16
NT = (((1,), (1,)), ((), ()))


def normalize(values, gain):
    center = jnp.mean(values, axis=-1, keepdims=True)
    moved = values - center
    spread = jnp.mean(jnp.square(moved), axis=-1, keepdims=True)
    return moved * lax.rsqrt(spread + 1e-05) * gain


def kernel(rows_count, cols_count, *refs):
    hbm, out_ref = refs[:12], refs[12]
    (
        slab_ref,
        pair_ref,
        mask_ref,
        gain_ref,
        wq_ref,
        wk_ref,
        wv_ref,
        wg_ref,
        gate_bias_ref,
        wb_ref,
        wo_ref,
        out_bias_ref,
    ) = local = refs[13:25]
    (
        slab_f32,
        slab_send,
        slab_recv,
        bias,
        chunk_f32,
        query,
        key,
        value_t,
        gate,
        shift,
        back_send,
        back_recv,
        in_sem,
        slab_ss,
        slab_rs,
        line_ss,
        line_rs,
        plane_ss,
        plane_rs,
        core_ss,
        core_rs,
        back_ss,
        back_rs,
    ) = refs[25:]
    devices = rows_count * cols_count
    tok, width, channels = slab_ref.shape
    key_blk, query_blk, _ = pair_ref.shape
    heads = wb_ref.shape[0]
    head_dim = channels // heads
    cols = width // devices
    tokens = devices * tok
    lanes = heads * query_blk
    owners = query_blk // tok
    scale = 1.0 / math.sqrt(head_dim)
    cores = 2
    line = cols_count // cores
    group = 2 - line % 2
    phases = 2 - cols % 2
    per = cols // phases
    my_row, my_col = lax.axis_index("row"), lax.axis_index("col")
    my_line, core = lax.div(my_col, cores), lax.rem(my_col, cores)
    me = my_row * cols_count + my_col

    def fetch(i):
        return pltpu.make_async_copy(hbm[i], local[i], in_sem.at[i])

    for i in (0, 3, 1, 9, 2, 4, 5, 6, 7, 8, 10, 11):
        fetch(i).start()

    def place(p):
        return (lax.div(p, cols_count), lax.rem(p, cols_count))

    def wait_bytes(ref, sem):
        pltpu.make_async_copy(ref, ref, sem).wait()

    def send(src, dst, send_sem, recv_sem, target):
        pltpu.make_async_remote_copy(
            src_ref=src,
            dst_ref=dst,
            send_sem=send_sem,
            recv_sem=recv_sem,
            device_id=target,
            device_id_type=MESH,
        ).start()

    barrier = pltpu.get_barrier_semaphore()

    def each_peer(act):
        def step(n, carry):
            r = lax.rem(my_row + n, rows_count)
            for m in range(cols_count):
                c = lax.rem(my_col + m, cols_count)
                if m:
                    act(r * cols_count + c, (r, c))
                else:

                    @pl.when(n > 0)
                    def _():
                        act(r * cols_count + c, (r, c))

            return carry

        lax.fori_loop(0, rows_count, step, 0)

    def greet(p, target):
        pl.semaphore_signal(barrier, inc=1, device_id=target, device_id_type=MESH)

    each_peer(greet)

    fetch(0).wait()
    fetch(3).wait()
    gain = gain_ref[...]
    for t in range(tok):
        slab_f32[t * width : (t + 1) * width, :] = normalize(slab_ref[t].astype(F32), gain)
    for p in range(devices):
        for f in range(phases):
            starts = [p * cols + f * per + jj for jj in range(per)]
            parts = [slab_f32[pl.ds(start, tok, stride=width), :] for start in starts]
            slab_send[f, p] = jnp.concatenate(parts, axis=0).astype(BF16)
    for f in range(phases):
        slab_recv[f, me] = slab_send[f, me]
    pl.semaphore_wait(barrier, devices - 1)

    def send_slab(f):
        def act(p, target):
            send(slab_send.at[f, p], slab_recv.at[f, me], slab_ss, slab_rs.at[f], target)

        each_peer(act)

    send_slab(0)

    fetch(1).wait()
    fetch(9).wait()
    lane_head = lax.broadcasted_iota(jnp.int32, (heads, lanes), 1) // query_blk
    spread_mat = (lane_head == lax.broadcasted_iota(jnp.int32, (heads, lanes), 0)).astype(F32)
    wide = lax.dot_general(
        wb_ref[...],
        spread_mat.astype(BF16),
        (((0,), (0,)), ((), ())),
        preferred_element_type=F32,
    ).astype(BF16)
    part = 16
    lane_query = lax.rem(lax.broadcasted_iota(jnp.int32, (part, query_blk, lanes), 2), query_blk)
    own_query = lane_query == lax.broadcasted_iota(jnp.int32, (part, query_blk, lanes), 1)
    for k in range(0, key_blk, part):
        rows = pair_ref[k : k + part].astype(F32).reshape(part * query_blk, channels)
        normed = normalize(rows, gain).astype(BF16)
        spread = jnp.dot(normed, wide, preferred_element_type=F32)
        spread = jnp.where(own_query, spread.reshape(part, query_blk, lanes), 0.0)
        bias[core, my_row, my_line, k : k + part, :] = jnp.sum(spread, axis=1).astype(BF16)
    for n in range(1, line):
        z = lax.rem(my_line + n, line)
        tile = bias.at[core, my_row, my_line]
        send(tile, tile, line_ss, line_rs, (my_row, z * cores + core))

    for f in range(1, phases):
        send_slab(f)

    wait_bytes(bias.at[core, my_row, pl.ds(0, line - 1)], line_rs)
    block = bias.at[core, my_row]
    for n in range(1, rows_count):
        r = lax.rem(my_row + n, rows_count)
        send(block, block, plane_ss, plane_rs, (r, my_col))
    send(block, block, core_ss, core_rs, (my_row, my_col + 1 - 2 * core))

    for i in (2, 4, 5, 6, 7, 8, 10, 11):
        fetch(i).wait()
    weights_qkg = jnp.concatenate([wq_ref[...], wk_ref[...], wg_ref[...]], axis=1)
    value_w = wv_ref[...].astype(F32).T.astype(BF16)

    def project(f):
        wait_bytes(slab_recv.at[f, pl.ds(0, devices - 1)], slab_rs.at[f])
        chunk_f32[...] = slab_recv[f].astype(F32)
        for j in range(per):
            jj = f * per + j
            rows = chunk_f32[:, j * tok : (j + 1) * tok, :].reshape(tokens, channels).astype(BF16)
            value_t[jj] = lax.dot_general(
                value_w, rows, NT, preferred_element_type=F32
            ).astype(BF16)
            joined = jnp.dot(rows, weights_qkg, preferred_element_type=F32)
            query[jj] = joined[:, :channels].astype(BF16)
            key[jj] = joined[:, channels : 2 * channels].astype(BF16)
            gate[jj] = jax.nn.sigmoid(joined[:, 2 * channels :] + gate_bias_ref[...])

    shift_row = (mask_ref[...].astype(F32) - 1.0) * 1000000000.0
    shift[...] = jnp.broadcast_to(shift_row, (lanes, tokens)).T
    project(0)

    wait_bytes(bias.at[core, pl.ds(0, rows_count - 1)], plane_rs)
    for n in range(1, rows_count):
        other = bias.at[core, lax.rem(my_row + n, rows_count)]
        send(other, other, core_ss, core_rs, (my_row, my_col + 1 - 2 * core))

    row_head = lax.broadcasted_iota(jnp.int32, (lanes, channels), 0) // query_blk
    chan_head = lax.broadcasted_iota(jnp.int32, (lanes, channels), 1) // head_dim
    own_head = row_head == chan_head

    def attend_block(f, half, z):
        c = z * cores + half
        bias_f32 = bias[half, :, z].astype(F32).reshape(tokens, lanes)
        at = pl.multiple_of(c * query_blk, query_blk)
        hidden = []
        for j in range(per):
            jj = f * per + j
            q_rows = query[jj, pl.ds(at, query_blk), :].astype(F32)
            q_heads = jnp.where(
                own_head, jnp.concatenate([q_rows] * heads, axis=0), 0.0
            ).astype(BF16)
            scores = lax.dot_general(key[jj], q_heads, NT, preferred_element_type=F32) * scale
            scores = (scores + bias_f32) + shift[...]
            top = jnp.max(scores, axis=0, keepdims=True)
            weights = jnp.exp(scores - top)
            denom = jnp.sum(weights, axis=0, keepdims=True)
            numer = jnp.dot(value_t[jj], weights.astype(BF16), preferred_element_type=F32)
            spread = jnp.where(own_head, (numer * (1.0 / denom)).T, 0.0)
            attended = spread[:query_blk]
            for h in range(1, heads):
                attended = attended + spread[h * query_blk : (h + 1) * query_blk]
            hidden.append((gate[jj, pl.ds(at, query_blk), :] * attended).astype(BF16))
        update = (
            jnp.dot(jnp.concatenate(hidden, axis=0), wo_ref[...], preferred_element_type=F32)
            + out_bias_ref[...]
        )
        for o in range(owners):
            starts = [j * query_blk + o * tok for j in range(per)]
            back_send[f, c * owners + o] = jnp.concatenate(
                [update[start : start + tok] for start in starts], axis=0
            ).astype(BF16)

    def send_back(f, half, z):
        for o in range(owners):
            p = (z * cores + half) * owners + o

            @pl.when(p != me)
            def _():
                send(back_send.at[f, p], back_recv.at[f, me], back_ss, back_rs, place(p))

    def attend_half(f, half):
        def step(n, carry):
            first = lax.rem(lax.div(my_line, group) + n, line // group) * group
            for m in range(group):
                attend_block(f, half, first + m)
            for m in range(group):
                send_back(f, half, first + m)
            return carry

        lax.fori_loop(0, line // group, step, 0)

    attend_half(0, core)
    wait_bytes(bias.at[1 - core], core_rs)
    attend_half(0, 1 - core)
    for f in range(1, phases):
        project(f)
        attend_half(f, core)
        attend_half(f, 1 - core)
    for f in range(phases):
        back_recv[f, me] = back_send[f, me]

    wait_bytes(slab_send.at[:, pl.ds(0, devices - 1)], slab_ss)
    wait_bytes(bias.at[core, my_row, pl.ds(0, line - 1)], line_ss)
    wait_bytes(bias.at[core, pl.ds(0, rows_count - 1)], plane_ss)
    wait_bytes(bias.at[core], core_ss)
    wait_bytes(back_send.at[:, pl.ds(0, devices - 1)], back_ss)
    wait_bytes(back_recv.at[:, pl.ds(0, devices - 1)], back_rs)
    slab_f32[...] = jnp.stack([back_recv[f] for f in range(phases)], axis=1).astype(F32).reshape(
        width * tok, channels
    )
    for t in range(tok):
        out_ref[t] = slab_f32[pl.ds(t, width, stride=tok), :].astype(BF16)


def per_device(
    slab, pair, mask, ln_gain, w_query, w_key, w_value, w_gate, gate_bias, w_bias, w_out, out_bias
):
    rows_count = lax.axis_size("row")
    cols_count = lax.axis_size("col")
    devices = rows_count * cols_count
    tok, width, channels = slab.shape
    key_blk, query_blk, _ = pair.shape
    heads = w_bias.shape[1]
    cols = width // devices
    tokens = devices * tok
    lanes = heads * query_blk
    phases = 2 - cols % 2
    rows = cols // phases * tok
    operands = (
        slab,
        pair,
        mask.reshape(1, -1),
        ln_gain.reshape(1, -1),
        w_query,
        w_key,
        w_value,
        w_gate,
        gate_bias.reshape(1, -1),
        w_bias.T,
        w_out,
        out_bias.reshape(1, -1),
    )
    dma = pltpu.SemaphoreType.DMA
    vmem = pltpu.VMEM
    return pl.pallas_call(
        functools.partial(kernel, rows_count, cols_count),
        out_shape=jax.ShapeDtypeStruct(slab.shape, BF16),
        in_specs=[pl.BlockSpec(memory_space=pltpu.HBM)] * len(operands),
        out_specs=pl.BlockSpec(memory_space=vmem),
        scratch_shapes=[vmem(x.shape, x.dtype) for x in operands]
        + [
            vmem((tok * width, channels), F32),
            vmem((phases, devices, rows, channels), BF16),
            vmem((phases, devices, rows, channels), BF16),
            vmem((2, rows_count, cols_count // 2, key_blk, lanes), BF16),
            vmem((devices, rows, channels), F32),
            vmem((cols, tokens, channels), BF16),
            vmem((cols, tokens, channels), BF16),
            vmem((cols, channels, tokens), BF16),
            vmem((cols, tokens, channels), F32),
            vmem((tokens, lanes), F32),
            vmem((phases, devices, rows, channels), BF16),
            vmem((phases, devices, rows, channels), BF16),
            dma((len(operands),)),
        ]
        + [dma, dma((phases,))]
        + [dma] * 8,
        compiler_params=pltpu.CompilerParams(
            collective_id=0, has_side_effects=True, vmem_limit_bytes=56 * 1024 * 1024
        ),
        cost_estimate=pl.CostEstimate(
            flops=2 * tokens * tokens * heads * channels * cols * 2,
            bytes_accessed=4 * slab.size,
            transcendentals=tokens * tokens * heads * cols,
        ),
        name="triangle",
    )(*operands)


def solution(mesh):
    placed = (P(("row", "col"), None, None), P("row", "col", None)) + (P(),) * 10
    return jax.shard_map(
        per_device,
        mesh=mesh,
        in_specs=placed,
        out_specs=P(("row", "col"), None, None),
        check_vma=False,
    )
```

```python
import functools
import math

import jax
import jax.numpy as jnp
from jax import lax
from jax.experimental import pallas as pl
from jax.experimental.pallas import tpu as pltpu
from jax.sharding import PartitionSpec as P

MESH = pl.DeviceIdType.MESH
F32 = jnp.float32
BF16 = jnp.bfloat16


def normalize(values, gain):
    center = jnp.mean(values, axis=-1, keepdims=True)
    moved = values - center
    spread = jnp.mean(jnp.square(moved), axis=-1, keepdims=True)
    return moved * lax.rsqrt(spread + 1e-05) * gain


def kernel(rows_count, cols_count, *refs):
    hbm, out_ref = refs[:12], refs[12]
    (
        slab_ref,
        pair_ref,
        mask_ref,
        gain_ref,
        wq_ref,
        wk_ref,
        wv_ref,
        wg_ref,
        gate_bias_ref,
        wb_ref,
        wo_ref,
        out_bias_ref,
    ) = local = refs[13:25]
    (
        slab_f32,
        slab_send,
        slab_recv,
        bias,
        chunk_f32,
        query,
        key_t,
        value,
        gate,
        bias_t,
        back_send,
        back_recv,
        in_sem,
        slab_ss,
        slab_rs,
        line_ss,
        line_rs,
        plane_ss,
        plane_rs,
        core_ss,
        core_rs,
        back_ss,
        back_rs,
    ) = refs[25:]
    devices = rows_count * cols_count
    tok, width, channels = slab_ref.shape
    key_blk, query_blk, _ = pair_ref.shape
    heads = wb_ref.shape[0]
    head_dim = channels // heads
    cols = width // devices
    tokens = devices * tok
    lanes = heads * query_blk
    owners = query_blk // tok
    scale = 1.0 / math.sqrt(head_dim)
    cores = 2
    line = cols_count // cores
    group = 2 - line % 2
    phases = 2 - cols % 2
    per = cols // phases
    my_row, my_col = lax.axis_index("row"), lax.axis_index("col")
    my_line, core = lax.div(my_col, cores), lax.rem(my_col, cores)
    me = my_row * cols_count + my_col

    def fetch(i):
        return pltpu.make_async_copy(hbm[i], local[i], in_sem.at[i])

    for i in (0, 3, 1, 9, 2, 4, 5, 6, 7, 8, 10, 11):
        fetch(i).start()

    def place(p):
        return (lax.div(p, cols_count), lax.rem(p, cols_count))

    def wait_bytes(ref, sem):
        pltpu.make_async_copy(ref, ref, sem).wait()

    def send(src, dst, send_sem, recv_sem, target):
        pltpu.make_async_remote_copy(
            src_ref=src,
            dst_ref=dst,
            send_sem=send_sem,
            recv_sem=recv_sem,
            device_id=target,
            device_id_type=MESH,
        ).start()

    barrier = pltpu.get_barrier_semaphore()

    def each_peer(act):
        def step(n, carry):
            r = lax.rem(my_row + n, rows_count)
            for m in range(cols_count):
                c = lax.rem(my_col + m, cols_count)
                if m:
                    act(r * cols_count + c, (r, c))
                else:

                    @pl.when(n > 0)
                    def _():
                        act(r * cols_count + c, (r, c))

            return carry

        lax.fori_loop(0, rows_count, step, 0)

    def greet(p, target):
        pl.semaphore_signal(barrier, inc=1, device_id=target, device_id_type=MESH)

    each_peer(greet)

    fetch(0).wait()
    fetch(3).wait()
    gain = gain_ref[...]
    for t in range(tok):
        slab_f32[t * width : (t + 1) * width, :] = normalize(slab_ref[t].astype(F32), gain)
    for p in range(devices):
        for f in range(phases):
            starts = [p * cols + f * per + jj for jj in range(per)]
            parts = [slab_f32[pl.ds(start, tok, stride=width), :] for start in starts]
            slab_send[f, p] = jnp.concatenate(parts, axis=0).astype(BF16)
    for f in range(phases):
        slab_recv[f, me] = slab_send[f, me]
    pl.semaphore_wait(barrier, devices - 1)

    def send_slab(f):
        def act(p, target):
            send(slab_send.at[f, p], slab_recv.at[f, me], slab_ss, slab_rs.at[f], target)

        each_peer(act)

    send_slab(0)

    fetch(1).wait()
    fetch(9).wait()
    lane_head = lax.broadcasted_iota(jnp.int32, (heads, lanes), 1) // query_blk
    spread_mat = (lane_head == lax.broadcasted_iota(jnp.int32, (heads, lanes), 0)).astype(F32)
    wide = lax.dot_general(
        wb_ref[...],
        spread_mat.astype(BF16),
        (((0,), (0,)), ((), ())),
        preferred_element_type=F32,
    ).astype(BF16)
    part = 16
    lane_query = lax.rem(lax.broadcasted_iota(jnp.int32, (part, query_blk, lanes), 2), query_blk)
    own_query = lane_query == lax.broadcasted_iota(jnp.int32, (part, query_blk, lanes), 1)
    for k in range(0, key_blk, part):
        rows = pair_ref[k : k + part].astype(F32).reshape(part * query_blk, channels)
        normed = normalize(rows, gain).astype(BF16)
        spread = jnp.dot(normed, wide, preferred_element_type=F32)
        spread = jnp.where(own_query, spread.reshape(part, query_blk, lanes), 0.0)
        bias[core, my_row, my_line, k : k + part, :] = jnp.sum(spread, axis=1).astype(BF16)
    for n in range(1, line):
        z = lax.rem(my_line + n, line)
        tile = bias.at[core, my_row, my_line]
        send(tile, tile, line_ss, line_rs, (my_row, z * cores + core))

    for f in range(1, phases):
        send_slab(f)

    wait_bytes(bias.at[core, my_row, pl.ds(0, line - 1)], line_rs)
    block = bias.at[core, my_row]
    for n in range(1, rows_count):
        r = lax.rem(my_row + n, rows_count)
        send(block, block, plane_ss, plane_rs, (r, my_col))
    send(block, block, core_ss, core_rs, (my_row, my_col + 1 - 2 * core))

    for i in (2, 4, 5, 6, 7, 8, 10, 11):
        fetch(i).wait()
    joined_w = jnp.concatenate([wq_ref[...], wk_ref[...], wv_ref[...], wg_ref[...]], axis=1)

    def project(f):
        wait_bytes(slab_recv.at[f, pl.ds(0, devices - 1)], slab_rs.at[f])
        chunk_f32[...] = slab_recv[f].astype(F32)
        for j in range(per):
            jj = f * per + j
            rows = chunk_f32[:, j * tok : (j + 1) * tok, :].reshape(tokens, channels).astype(BF16)
            joined = jnp.dot(rows, joined_w, preferred_element_type=F32)
            query[jj] = joined[:, :channels].astype(BF16)
            key_t[jj] = joined[:, channels : 2 * channels].T.astype(BF16)
            value[jj] = joined[:, 2 * channels : 3 * channels].astype(BF16)
            gate[jj] = jax.nn.sigmoid(joined[:, 3 * channels :] + gate_bias_ref[...])

    project(0)

    wait_bytes(bias.at[core, pl.ds(0, rows_count - 1)], plane_rs)
    for n in range(1, rows_count):
        other = bias.at[core, lax.rem(my_row + n, rows_count)]
        send(other, other, core_ss, core_rs, (my_row, my_col + 1 - 2 * core))

    row_head = lax.broadcasted_iota(jnp.int32, (group * lanes, channels), 0) // query_blk
    chan_head = lax.broadcasted_iota(jnp.int32, (group * lanes, channels), 1) // head_dim
    own_head = lax.rem(row_head, heads) == chan_head
    shift = (mask_ref[...].astype(F32) - 1.0) * 1000000000.0

    def turn_bias(half):
        def step(z, carry):
            bias_t[half, z] = bias[half, :, z].astype(F32).reshape(tokens, lanes).T
            return carry

        lax.fori_loop(0, line, step, 0)

    def attend_blocks(f, half, z):
        at = [
            pl.multiple_of(((z + m) * cores + half) * query_blk, query_blk) for m in range(group)
        ]
        bias_rows = bias_t[half, pl.ds(z, group)].reshape(group * lanes, tokens)
        every = range(f * per, f * per + per)
        scores = []
        for jj in every:
            copies = []
            for m in range(group):
                copies += [query[jj, pl.ds(at[m], query_blk), :].astype(F32)] * heads
            q_heads = jnp.where(own_head, jnp.concatenate(copies, axis=0), 0.0).astype(BF16)
            scores.append(jnp.dot(q_heads, key_t[jj], preferred_element_type=F32))
        scores = [(x * scale + bias_rows) + shift for x in scores]
        tops = [jnp.max(x, axis=1, keepdims=True) for x in scores]
        weights = [jnp.exp(x - top) for x, top in zip(scores, tops)]
        denoms = [jnp.sum(x, axis=1, keepdims=True) for x in weights]
        numers = [
            jnp.dot(x.astype(BF16), value[jj], preferred_element_type=F32)
            for x, jj in zip(weights, every)
        ]
        hidden = []
        for numer, denom, jj in zip(numers, denoms, every):
            spread = jnp.where(own_head, numer * (1.0 / denom), 0.0)
            for m in range(group):
                base = m * lanes
                attended = spread[base : base + query_blk]
                for h in range(1, heads):
                    start = base + h * query_blk
                    attended = attended + spread[start : start + query_blk]
                hidden.append((gate[jj, pl.ds(at[m], query_blk), :] * attended).astype(BF16))
        update = (
            jnp.dot(jnp.concatenate(hidden, axis=0), wo_ref[...], preferred_element_type=F32)
            + out_bias_ref[...]
        )
        for m in range(group):
            for o in range(owners):
                starts = [(j * group + m) * query_blk + o * tok for j in range(per)]
                back_send[f, ((z + m) * cores + half) * owners + o] = jnp.concatenate(
                    [update[start : start + tok] for start in starts], axis=0
                ).astype(BF16)

    def send_back(f, half, z):
        for o in range(owners):
            p = (z * cores + half) * owners + o

            @pl.when(p != me)
            def _():
                send(back_send.at[f, p], back_recv.at[f, me], back_ss, back_rs, place(p))

    def attend_half(f, half):
        def step(n, carry):
            first = lax.rem(lax.div(my_line, group) + n, line // group) * group
            attend_blocks(f, half, first)
            for m in range(group):
                send_back(f, half, first + m)
            return carry

        lax.fori_loop(0, line // group, step, 0)

    turn_bias(core)
    attend_half(0, core)
    wait_bytes(bias.at[1 - core], core_rs)
    turn_bias(1 - core)
    attend_half(0, 1 - core)
    for f in range(1, phases):
        project(f)
        attend_half(f, core)
        attend_half(f, 1 - core)
    for f in range(phases):
        back_recv[f, me] = back_send[f, me]

    wait_bytes(slab_send.at[:, pl.ds(0, devices - 1)], slab_ss)
    wait_bytes(bias.at[core, my_row, pl.ds(0, line - 1)], line_ss)
    wait_bytes(bias.at[core, pl.ds(0, rows_count - 1)], plane_ss)
    wait_bytes(bias.at[core], core_ss)
    wait_bytes(back_send.at[:, pl.ds(0, devices - 1)], back_ss)
    wait_bytes(back_recv.at[:, pl.ds(0, devices - 1)], back_rs)
    slab_f32[...] = jnp.stack([back_recv[f] for f in range(phases)], axis=1).astype(F32).reshape(
        width * tok, channels
    )
    for t in range(tok):
        out_ref[t] = slab_f32[pl.ds(t, width, stride=tok), :].astype(BF16)


def per_device(
    slab, pair, mask, ln_gain, w_query, w_key, w_value, w_gate, gate_bias, w_bias, w_out, out_bias
):
    rows_count = lax.axis_size("row")
    cols_count = lax.axis_size("col")
    devices = rows_count * cols_count
    tok, width, channels = slab.shape
    key_blk, query_blk, _ = pair.shape
    heads = w_bias.shape[1]
    cols = width // devices
    tokens = devices * tok
    lanes = heads * query_blk
    phases = 2 - cols % 2
    rows = cols // phases * tok
    operands = (
        slab,
        pair,
        mask.reshape(1, -1),
        ln_gain.reshape(1, -1),
        w_query,
        w_key,
        w_value,
        w_gate,
        gate_bias.reshape(1, -1),
        w_bias.T,
        w_out,
        out_bias.reshape(1, -1),
    )
    dma = pltpu.SemaphoreType.DMA
    vmem = pltpu.VMEM
    return pl.pallas_call(
        functools.partial(kernel, rows_count, cols_count),
        out_shape=jax.ShapeDtypeStruct(slab.shape, BF16),
        in_specs=[pl.BlockSpec(memory_space=pltpu.HBM)] * len(operands),
        out_specs=pl.BlockSpec(memory_space=vmem),
        scratch_shapes=[vmem(x.shape, x.dtype) for x in operands]
        + [
            vmem((tok * width, channels), F32),
            vmem((phases, devices, rows, channels), BF16),
            vmem((phases, devices, rows, channels), BF16),
            vmem((2, rows_count, cols_count // 2, key_blk, lanes), BF16),
            vmem((devices, rows, channels), F32),
            vmem((cols, tokens, channels), BF16),
            vmem((cols, channels, tokens), BF16),
            vmem((cols, tokens, channels), BF16),
            vmem((cols, tokens, channels), F32),
            vmem((2, cols_count // 2, lanes, tokens), F32),
            vmem((phases, devices, rows, channels), BF16),
            vmem((phases, devices, rows, channels), BF16),
            dma((len(operands),)),
        ]
        + [dma, dma((phases,))]
        + [dma] * 8,
        compiler_params=pltpu.CompilerParams(
            collective_id=0, has_side_effects=True, vmem_limit_bytes=56 * 1024 * 1024
        ),
        cost_estimate=pl.CostEstimate(
            flops=2 * tokens * tokens * heads * channels * cols * 2,
            bytes_accessed=4 * slab.size,
            transcendentals=tokens * tokens * heads * cols,
        ),
        name="triangle",
    )(*operands)


def solution(mesh):
    placed = (P(("row", "col"), None, None), P("row", "col", None)) + (P(),) * 10
    return jax.shard_map(
        per_device,
        mesh=mesh,
        in_specs=placed,
        out_specs=P(("row", "col"), None, None),
        check_vma=False,
    )
```

```python
import functools
import math

import jax
import jax.numpy as jnp
from jax import lax
from jax.experimental import pallas as pl
from jax.experimental.pallas import tpu as pltpu
from jax.sharding import PartitionSpec as P

MESH = pl.DeviceIdType.MESH
F32 = jnp.float32
BF16 = jnp.bfloat16


def normalize(values, gain):
    center = jnp.mean(values, axis=-1, keepdims=True)
    moved = values - center
    spread = jnp.mean(jnp.square(moved), axis=-1, keepdims=True)
    return moved * lax.rsqrt(spread + 1e-05) * gain


def kernel(rows_count, cols_count, *refs):
    hbm, out_ref = refs[:12], refs[12]
    (
        slab_ref,
        pair_ref,
        mask_ref,
        gain_ref,
        wq_ref,
        wk_ref,
        wv_ref,
        wg_ref,
        gate_bias_ref,
        wb_ref,
        wo_ref,
        out_bias_ref,
    ) = local = refs[13:25]
    (
        slab_f32,
        slab_send,
        slab_recv,
        bias,
        chunk_f32,
        query,
        key_t,
        value,
        gate,
        bias_t,
        back_send,
        back_recv,
        in_sem,
        slab_ss,
        slab_rs,
        line_ss,
        line_rs,
        plane_ss,
        plane_rs,
        core_ss,
        core_rs,
        back_ss,
        back_rs,
    ) = refs[25:]
    devices = rows_count * cols_count
    tok, width, channels = slab_ref.shape
    key_blk, query_blk, _ = pair_ref.shape
    heads = wb_ref.shape[0]
    head_dim = channels // heads
    cols = width // devices
    tokens = devices * tok
    lanes = heads * query_blk
    owners = query_blk // tok
    scale = 1.0 / math.sqrt(head_dim)
    cores = 2
    line = cols_count // cores
    group = 2 - line % 2
    phases = 1
    per = cols // phases
    my_row, my_col = lax.axis_index("row"), lax.axis_index("col")
    my_line, core = lax.div(my_col, cores), lax.rem(my_col, cores)
    me = my_row * cols_count + my_col

    def fetch(i):
        return pltpu.make_async_copy(hbm[i], local[i], in_sem.at[i])

    for i in (0, 3, 1, 9, 2, 4, 5, 6, 7, 8, 10, 11):
        fetch(i).start()

    def place(p):
        return (lax.div(p, cols_count), lax.rem(p, cols_count))

    def wait_bytes(ref, sem):
        pltpu.make_async_copy(ref, ref, sem).wait()

    def send(src, dst, send_sem, recv_sem, target):
        pltpu.make_async_remote_copy(
            src_ref=src,
            dst_ref=dst,
            send_sem=send_sem,
            recv_sem=recv_sem,
            device_id=target,
            device_id_type=MESH,
        ).start()

    barrier = pltpu.get_barrier_semaphore()

    def each_peer(act):
        def step(n, carry):
            r = lax.rem(my_row + n, rows_count)
            for m in range(cols_count):
                c = lax.rem(my_col + m, cols_count)
                if m:
                    act(r * cols_count + c, (r, c))
                else:

                    @pl.when(n > 0)
                    def _():
                        act(r * cols_count + c, (r, c))

            return carry

        lax.fori_loop(0, rows_count, step, 0)

    def greet(p, target):
        pl.semaphore_signal(barrier, inc=1, device_id=target, device_id_type=MESH)

    each_peer(greet)

    fetch(0).wait()
    fetch(3).wait()
    gain = gain_ref[...]
    for t in range(tok):
        slab_f32[t * width : (t + 1) * width, :] = normalize(slab_ref[t].astype(F32), gain)
    for p in range(devices):
        for f in range(phases):
            starts = [p * cols + f * per + jj for jj in range(per)]
            parts = [slab_f32[pl.ds(start, tok, stride=width), :] for start in starts]
            slab_send[f, p] = jnp.concatenate(parts, axis=0).astype(BF16)
    for f in range(phases):
        slab_recv[f, me] = slab_send[f, me]
    pl.semaphore_wait(barrier, devices - 1)

    def send_slab(f):
        def act(p, target):
            send(slab_send.at[f, p], slab_recv.at[f, me], slab_ss, slab_rs.at[f], target)

        each_peer(act)

    send_slab(0)

    fetch(1).wait()
    fetch(9).wait()
    lane_head = lax.broadcasted_iota(jnp.int32, (heads, lanes), 1) // query_blk
    spread_mat = (lane_head == lax.broadcasted_iota(jnp.int32, (heads, lanes), 0)).astype(F32)
    wide = lax.dot_general(
        wb_ref[...],
        spread_mat.astype(BF16),
        (((0,), (0,)), ((), ())),
        preferred_element_type=F32,
    ).astype(BF16)
    part = 16
    lane_query = lax.rem(lax.broadcasted_iota(jnp.int32, (part, query_blk, lanes), 2), query_blk)
    own_query = lane_query == lax.broadcasted_iota(jnp.int32, (part, query_blk, lanes), 1)
    for k in range(0, key_blk, part):
        rows = pair_ref[k : k + part].astype(F32).reshape(part * query_blk, channels)
        normed = normalize(rows, gain).astype(BF16)
        spread = jnp.dot(normed, wide, preferred_element_type=F32)
        spread = jnp.where(own_query, spread.reshape(part, query_blk, lanes), 0.0)
        bias[core, my_row, my_line, k : k + part, :] = jnp.sum(spread, axis=1).astype(BF16)
    for n in range(1, line):
        z = lax.rem(my_line + n, line)
        tile = bias.at[core, my_row, my_line]
        send(tile, tile, line_ss, line_rs, (my_row, z * cores + core))

    for f in range(1, phases):
        send_slab(f)

    wait_bytes(bias.at[core, my_row, pl.ds(0, line - 1)], line_rs)
    block = bias.at[core, my_row]
    for n in range(1, rows_count):
        r = lax.rem(my_row + n, rows_count)
        send(block, block, plane_ss, plane_rs, (r, my_col))
    send(block, block, core_ss, core_rs, (my_row, my_col + 1 - 2 * core))

    for i in (2, 4, 5, 6, 7, 8, 10, 11):
        fetch(i).wait()
    joined_w = jnp.concatenate([wq_ref[...], wk_ref[...], wv_ref[...], wg_ref[...]], axis=1)

    def project(f):
        wait_bytes(slab_recv.at[f, pl.ds(0, devices - 1)], slab_rs.at[f])
        chunk_f32[...] = slab_recv[f].astype(F32)
        for j in range(per):
            jj = f * per + j
            rows = chunk_f32[:, j * tok : (j + 1) * tok, :].reshape(tokens, channels).astype(BF16)
            joined = jnp.dot(rows, joined_w, preferred_element_type=F32)
            query[jj] = joined[:, :channels].astype(BF16)
            key_t[jj] = joined[:, channels : 2 * channels].T.astype(BF16)
            value[jj] = joined[:, 2 * channels : 3 * channels].astype(BF16)
            gate[jj] = jax.nn.sigmoid(joined[:, 3 * channels :] + gate_bias_ref[...])

    project(0)

    wait_bytes(bias.at[core, pl.ds(0, rows_count - 1)], plane_rs)
    for n in range(1, rows_count):
        other = bias.at[core, lax.rem(my_row + n, rows_count)]
        send(other, other, core_ss, core_rs, (my_row, my_col + 1 - 2 * core))

    row_head = lax.broadcasted_iota(jnp.int32, (group * lanes, channels), 0) // query_blk
    chan_head = lax.broadcasted_iota(jnp.int32, (group * lanes, channels), 1) // head_dim
    own_head = lax.rem(row_head, heads) == chan_head
    shift = (mask_ref[...].astype(F32) - 1.0) * 1000000000.0

    def turn_bias(half):
        def step(z, carry):
            bias_t[half, z] = bias[half, :, z].astype(F32).reshape(tokens, lanes).T
            return carry

        lax.fori_loop(0, line, step, 0)

    def attend_blocks(f, half, z):
        at = [
            pl.multiple_of(((z + m) * cores + half) * query_blk, query_blk) for m in range(group)
        ]
        bias_rows = bias_t[half, pl.ds(z, group)].reshape(group * lanes, tokens)
        every = range(f * per, f * per + per)
        scores = []
        for jj in every:
            copies = []
            for m in range(group):
                copies += [query[jj, pl.ds(at[m], query_blk), :].astype(F32)] * heads
            q_heads = jnp.where(own_head, jnp.concatenate(copies, axis=0), 0.0).astype(BF16)
            scores.append(jnp.dot(q_heads, key_t[jj], preferred_element_type=F32))
        scores = [(x * scale + bias_rows) + shift for x in scores]
        tops = [jnp.max(x, axis=1, keepdims=True) for x in scores]
        weights = [jnp.exp(x - top) for x, top in zip(scores, tops)]
        denoms = [jnp.sum(x, axis=1, keepdims=True) for x in weights]
        numers = [
            jnp.dot(x.astype(BF16), value[jj], preferred_element_type=F32)
            for x, jj in zip(weights, every)
        ]
        hidden = []
        for numer, denom, jj in zip(numers, denoms, every):
            spread = jnp.where(own_head, numer * (1.0 / denom), 0.0)
            for m in range(group):
                base = m * lanes
                attended = spread[base : base + query_blk]
                for h in range(1, heads):
                    start = base + h * query_blk
                    attended = attended + spread[start : start + query_blk]
                hidden.append((gate[jj, pl.ds(at[m], query_blk), :] * attended).astype(BF16))
        update = (
            jnp.dot(jnp.concatenate(hidden, axis=0), wo_ref[...], preferred_element_type=F32)
            + out_bias_ref[...]
        )
        for m in range(group):
            for o in range(owners):
                starts = [(j * group + m) * query_blk + o * tok for j in range(per)]
                back_send[f, ((z + m) * cores + half) * owners + o] = jnp.concatenate(
                    [update[start : start + tok] for start in starts], axis=0
                ).astype(BF16)

    def send_back(f, half, z):
        for o in range(owners):
            p = (z * cores + half) * owners + o

            @pl.when(p != me)
            def _():
                send(back_send.at[f, p], back_recv.at[f, me], back_ss, back_rs, place(p))

    def attend_half(f, half):
        def step(n, carry):
            first = lax.rem(lax.div(my_line, group) + n, line // group) * group
            attend_blocks(f, half, first)
            for m in range(group):
                send_back(f, half, first + m)
            return carry

        lax.fori_loop(0, line // group, step, 0)

    turn_bias(core)
    attend_half(0, core)
    wait_bytes(bias.at[1 - core], core_rs)
    turn_bias(1 - core)
    attend_half(0, 1 - core)
    for f in range(1, phases):
        project(f)
        attend_half(f, core)
        attend_half(f, 1 - core)
    for f in range(phases):
        back_recv[f, me] = back_send[f, me]

    wait_bytes(slab_send.at[:, pl.ds(0, devices - 1)], slab_ss)
    wait_bytes(bias.at[core, my_row, pl.ds(0, line - 1)], line_ss)
    wait_bytes(bias.at[core, pl.ds(0, rows_count - 1)], plane_ss)
    wait_bytes(bias.at[core], core_ss)
    wait_bytes(back_send.at[:, pl.ds(0, devices - 1)], back_ss)
    wait_bytes(back_recv.at[:, pl.ds(0, devices - 1)], back_rs)
    slab_f32[...] = jnp.stack([back_recv[f] for f in range(phases)], axis=1).astype(F32).reshape(
        width * tok, channels
    )
    for t in range(tok):
        out_ref[t] = slab_f32[pl.ds(t, width, stride=tok), :].astype(BF16)


def per_device(
    slab, pair, mask, ln_gain, w_query, w_key, w_value, w_gate, gate_bias, w_bias, w_out, out_bias
):
    rows_count = lax.axis_size("row")
    cols_count = lax.axis_size("col")
    devices = rows_count * cols_count
    tok, width, channels = slab.shape
    key_blk, query_blk, _ = pair.shape
    heads = w_bias.shape[1]
    cols = width // devices
    tokens = devices * tok
    lanes = heads * query_blk
    phases = 1
    rows = cols // phases * tok
    operands = (
        slab,
        pair,
        mask.reshape(1, -1),
        ln_gain.reshape(1, -1),
        w_query,
        w_key,
        w_value,
        w_gate,
        gate_bias.reshape(1, -1),
        w_bias.T,
        w_out,
        out_bias.reshape(1, -1),
    )
    dma = pltpu.SemaphoreType.DMA
    vmem = pltpu.VMEM
    return pl.pallas_call(
        functools.partial(kernel, rows_count, cols_count),
        out_shape=jax.ShapeDtypeStruct(slab.shape, BF16),
        in_specs=[pl.BlockSpec(memory_space=pltpu.HBM)] * len(operands),
        out_specs=pl.BlockSpec(memory_space=vmem),
        scratch_shapes=[vmem(x.shape, x.dtype) for x in operands]
        + [
            vmem((tok * width, channels), F32),
            vmem((phases, devices, rows, channels), BF16),
            vmem((phases, devices, rows, channels), BF16),
            vmem((2, rows_count, cols_count // 2, key_blk, lanes), BF16),
            vmem((devices, rows, channels), F32),
            vmem((cols, tokens, channels), BF16),
            vmem((cols, channels, tokens), BF16),
            vmem((cols, tokens, channels), BF16),
            vmem((cols, tokens, channels), F32),
            vmem((2, cols_count // 2, lanes, tokens), F32),
            vmem((phases, devices, rows, channels), BF16),
            vmem((phases, devices, rows, channels), BF16),
            dma((len(operands),)),
        ]
        + [dma, dma((phases,))]
        + [dma] * 8,
        compiler_params=pltpu.CompilerParams(
            collective_id=0, has_side_effects=True, vmem_limit_bytes=56 * 1024 * 1024
        ),
        cost_estimate=pl.CostEstimate(
            flops=2 * tokens * tokens * heads * channels * cols * 2,
            bytes_accessed=4 * slab.size,
            transcendentals=tokens * tokens * heads * cols,
        ),
        name="triangle",
    )(*operands)


def solution(mesh):
    placed = (P(("row", "col"), None, None), P("row", "col", None)) + (P(),) * 10
    return jax.shard_map(
        per_device,
        mesh=mesh,
        in_specs=placed,
        out_specs=P(("row", "col"), None, None),
        check_vma=False,
    )
```

```python
import functools
import math

import jax
import jax.numpy as jnp
from jax import lax
from jax.experimental import pallas as pl
from jax.experimental.pallas import tpu as pltpu
from jax.sharding import PartitionSpec as P

MESH = pl.DeviceIdType.MESH
F32 = jnp.float32
BF16 = jnp.bfloat16


def normalize(values, gain):
    center = jnp.mean(values, axis=-1, keepdims=True)
    moved = values - center
    spread = jnp.mean(jnp.square(moved), axis=-1, keepdims=True)
    return moved * lax.rsqrt(spread + 1e-05) * gain


def kernel(rows_count, cols_count, *refs):
    hbm, out_ref = refs[:12], refs[12]
    (
        slab_ref,
        pair_ref,
        mask_ref,
        gain_ref,
        wq_ref,
        wk_ref,
        wv_ref,
        wg_ref,
        gate_bias_ref,
        wb_ref,
        wo_ref,
        out_bias_ref,
    ) = local = refs[13:25]
    (
        slab_f32,
        slab_send,
        slab_recv,
        bias,
        chunk_f32,
        query,
        key_t,
        value,
        gate,
        bias_t,
        back_send,
        back_recv,
        in_sem,
        slab_ss,
        slab_rs,
        line_ss,
        line_rs,
        plane_ss,
        plane_rs,
        core_ss,
        core_rs,
        back_ss,
        back_rs,
    ) = refs[25:]
    devices = rows_count * cols_count
    tok, width, channels = slab_ref.shape
    key_blk, query_blk, _ = pair_ref.shape
    heads = wb_ref.shape[0]
    head_dim = channels // heads
    cols = width // devices
    tokens = devices * tok
    lanes = heads * query_blk
    owners = query_blk // tok
    scale = 1.0 / math.sqrt(head_dim)
    cores = 2
    line = cols_count // cores
    group = 2 - line % 2
    phases = 2 - cols % 2
    per = cols // phases
    my_row, my_col = lax.axis_index("row"), lax.axis_index("col")
    my_line, core = lax.div(my_col, cores), lax.rem(my_col, cores)
    me = my_row * cols_count + my_col

    def fetch(i):
        return pltpu.make_async_copy(hbm[i], local[i], in_sem.at[i])

    for i in (0, 3, 1, 9, 2, 4, 5, 6, 7, 8, 10, 11):
        fetch(i).start()

    def place(p):
        return (lax.div(p, cols_count), lax.rem(p, cols_count))

    def wait_bytes(ref, sem):
        pltpu.make_async_copy(ref, ref, sem).wait()

    def send(src, dst, send_sem, recv_sem, target):
        pltpu.make_async_remote_copy(
            src_ref=src,
            dst_ref=dst,
            send_sem=send_sem,
            recv_sem=recv_sem,
            device_id=target,
            device_id_type=MESH,
        ).start()

    barrier = pltpu.get_barrier_semaphore()

    def each_peer(act):
        def step(n, carry):
            r = lax.rem(my_row + n, rows_count)
            for m in range(cols_count):
                c = lax.rem(my_col + m, cols_count)
                if m:
                    act(r * cols_count + c, (r, c))
                else:

                    @pl.when(n > 0)
                    def _():
                        act(r * cols_count + c, (r, c))

            return carry

        lax.fori_loop(0, rows_count, step, 0)

    def greet(p, target):
        pl.semaphore_signal(barrier, inc=1, device_id=target, device_id_type=MESH)

    each_peer(greet)

    fetch(0).wait()
    fetch(3).wait()
    gain = gain_ref[...]
    flat = slab_f32.reshape(width * tok, channels)
    for t in range(tok):
        flat[t * width : (t + 1) * width, :] = normalize(slab_ref[t].astype(F32), gain)
    def cut_slab(f):
        for p in range(devices):
            starts = [p * cols + f * per + jj for jj in range(per)]
            parts = [flat[pl.ds(start, tok, stride=width), :] for start in starts]
            slab_send[f, p] = jnp.concatenate(parts, axis=0).astype(BF16)
        slab_recv[f, me] = slab_send[f, me]

    cut_slab(0)
    pl.semaphore_wait(barrier, devices - 1)

    def send_slab(f):
        def act(p, target):
            send(slab_send.at[f, p], slab_recv.at[f, me], slab_ss, slab_rs.at[f], target)

        each_peer(act)

    send_slab(0)

    fetch(1).wait()
    fetch(9).wait()
    lane_head = lax.broadcasted_iota(jnp.int32, (heads, lanes), 1) // query_blk
    spread_mat = (lane_head == lax.broadcasted_iota(jnp.int32, (heads, lanes), 0)).astype(F32)
    wide = lax.dot_general(
        wb_ref[...],
        spread_mat.astype(BF16),
        (((0,), (0,)), ((), ())),
        preferred_element_type=F32,
    ).astype(BF16)
    part = 16
    lane_query = lax.rem(lax.broadcasted_iota(jnp.int32, (part, query_blk, lanes), 2), query_blk)
    own_query = lane_query == lax.broadcasted_iota(jnp.int32, (part, query_blk, lanes), 1)
    for k in range(0, key_blk, part):
        rows = pair_ref[k : k + part].astype(F32).reshape(part * query_blk, channels)
        normed = normalize(rows, gain).astype(BF16)
        spread = jnp.dot(normed, wide, preferred_element_type=F32)
        spread = jnp.where(own_query, spread.reshape(part, query_blk, lanes), 0.0)
        bias[core, my_row, my_line, k : k + part, :] = jnp.sum(spread, axis=1).astype(BF16)
    for n in range(1, line):
        z = lax.rem(my_line + n, line)
        tile = bias.at[core, my_row, my_line]
        send(tile, tile, line_ss, line_rs, (my_row, z * cores + core))

    for f in range(1, phases):
        cut_slab(f)
        send_slab(f)

    wait_bytes(bias.at[core, my_row, pl.ds(0, line - 1)], line_rs)
    block = bias.at[core, my_row]
    for n in range(1, rows_count):
        r = lax.rem(my_row + n, rows_count)
        send(block, block, plane_ss, plane_rs, (r, my_col))
    send(block, block, core_ss, core_rs, (my_row, my_col + 1 - 2 * core))

    for i in (2, 4, 5, 6, 7, 8, 10, 11):
        fetch(i).wait()
    joined_w = jnp.concatenate([wq_ref[...], wk_ref[...], wv_ref[...], wg_ref[...]], axis=1)

    def project(f):
        wait_bytes(slab_recv.at[f, pl.ds(0, devices - 1)], slab_rs.at[f])
        chunk_f32[...] = slab_recv[f].astype(F32)
        for j in range(per):
            jj = f * per + j
            rows = chunk_f32[:, j * tok : (j + 1) * tok, :].reshape(tokens, channels).astype(BF16)
            joined = jnp.dot(rows, joined_w, preferred_element_type=F32)
            query[jj] = joined[:, :channels].astype(BF16)
            key_t[jj] = joined[:, channels : 2 * channels].T.astype(BF16)
            value[jj] = joined[:, 2 * channels : 3 * channels].astype(BF16)
            gate[jj] = jax.nn.sigmoid(joined[:, 3 * channels :] + gate_bias_ref[...])

    project(0)

    wait_bytes(bias.at[core, pl.ds(0, rows_count - 1)], plane_rs)
    for n in range(1, rows_count):
        other = bias.at[core, lax.rem(my_row + n, rows_count)]
        send(other, other, core_ss, core_rs, (my_row, my_col + 1 - 2 * core))

    row_head = lax.broadcasted_iota(jnp.int32, (group * lanes, channels), 0) // query_blk
    chan_head = lax.broadcasted_iota(jnp.int32, (group * lanes, channels), 1) // head_dim
    own_head = lax.rem(row_head, heads) == chan_head
    shift = (mask_ref[...].astype(F32) - 1.0) * 1000000000.0

    def turn_bias(half):
        def step(z, carry):
            bias_t[half, z] = bias[half, :, z].astype(F32).reshape(tokens, lanes).T
            return carry

        lax.fori_loop(0, line, step, 0)

    def attend_blocks(f, half, z):
        at = [
            pl.multiple_of(((z + m) * cores + half) * query_blk, query_blk) for m in range(group)
        ]
        bias_rows = bias_t[half, pl.ds(z, group)].reshape(group * lanes, tokens)
        every = range(f * per, f * per + per)
        scores = []
        for jj in every:
            copies = []
            for m in range(group):
                copies += [query[jj, pl.ds(at[m], query_blk), :].astype(F32)] * heads
            q_heads = jnp.where(own_head, jnp.concatenate(copies, axis=0), 0.0).astype(BF16)
            scores.append(jnp.dot(q_heads, key_t[jj], preferred_element_type=F32))
        scores = [(x * scale + bias_rows) + shift for x in scores]
        tops = [jnp.max(x, axis=1, keepdims=True) for x in scores]
        weights = [jnp.exp(x - top) for x, top in zip(scores, tops)]
        denoms = [jnp.sum(x, axis=1, keepdims=True) for x in weights]
        numers = [
            jnp.dot(x.astype(BF16), value[jj], preferred_element_type=F32)
            for x, jj in zip(weights, every)
        ]
        hidden = []
        for numer, denom, jj in zip(numers, denoms, every):
            spread = jnp.where(own_head, numer * (1.0 / denom), 0.0)
            for m in range(group):
                base = m * lanes
                attended = spread[base : base + query_blk]
                for h in range(1, heads):
                    start = base + h * query_blk
                    attended = attended + spread[start : start + query_blk]
                hidden.append((gate[jj, pl.ds(at[m], query_blk), :] * attended).astype(BF16))
        update = (
            jnp.dot(jnp.concatenate(hidden, axis=0), wo_ref[...], preferred_element_type=F32)
            + out_bias_ref[...]
        )
        for m in range(group):
            for o in range(owners):
                starts = [(j * group + m) * query_blk + o * tok for j in range(per)]
                back_send[f, ((z + m) * cores + half) * owners + o] = jnp.concatenate(
                    [update[start : start + tok] for start in starts], axis=0
                ).astype(BF16)

    def send_back(f, half, z):
        for o in range(owners):
            p = (z * cores + half) * owners + o

            @pl.when(p != me)
            def _():
                send(back_send.at[f, p], back_recv.at[f, me], back_ss, back_rs.at[f], place(p))

    def attend_half(f, half):
        firsts = [
            lax.rem(lax.div(my_line, group) + n, line // group) * group
            for n in range(line // group)
        ]
        width_z = min(2, len(firsts))
        for base in range(0, len(firsts), width_z):
            some = firsts[base : base + width_z]
            for first in some:
                attend_blocks(f, half, first)
            for first in some:
                for m in range(group):
                    send_back(f, half, first + m)

    turn_bias(core)
    attend_half(0, core)
    wait_bytes(bias.at[1 - core], core_rs)
    turn_bias(1 - core)
    attend_half(0, 1 - core)
    for f in range(1, phases):
        project(f)
        attend_half(f, core)
        attend_half(f, 1 - core)
    for f in range(phases):
        back_recv[f, me] = back_send[f, me]

    wait_bytes(slab_send.at[:, pl.ds(0, devices - 1)], slab_ss)
    wait_bytes(bias.at[core, my_row, pl.ds(0, line - 1)], line_ss)
    wait_bytes(bias.at[core, pl.ds(0, rows_count - 1)], plane_ss)
    wait_bytes(bias.at[core], core_ss)
    wait_bytes(back_send.at[:, pl.ds(0, devices - 1)], back_ss)
    for f in range(phases):
        wait_bytes(back_recv.at[f, pl.ds(0, devices - 1)], back_rs.at[f])
        slab_f32[:, f] = back_recv[f].astype(F32)
    for t in range(tok):
        out_ref[t] = flat[pl.ds(t, width, stride=tok), :].astype(BF16)


def per_device(
    slab, pair, mask, ln_gain, w_query, w_key, w_value, w_gate, gate_bias, w_bias, w_out, out_bias
):
    rows_count = lax.axis_size("row")
    cols_count = lax.axis_size("col")
    devices = rows_count * cols_count
    tok, width, channels = slab.shape
    key_blk, query_blk, _ = pair.shape
    heads = w_bias.shape[1]
    cols = width // devices
    tokens = devices * tok
    lanes = heads * query_blk
    phases = 2 - cols % 2
    rows = cols // phases * tok
    operands = (
        slab,
        pair,
        mask.reshape(1, -1),
        ln_gain.reshape(1, -1),
        w_query,
        w_key,
        w_value,
        w_gate,
        gate_bias.reshape(1, -1),
        w_bias.T,
        w_out,
        out_bias.reshape(1, -1),
    )
    dma = pltpu.SemaphoreType.DMA
    vmem = pltpu.VMEM
    return pl.pallas_call(
        functools.partial(kernel, rows_count, cols_count),
        out_shape=jax.ShapeDtypeStruct(slab.shape, BF16),
        in_specs=[pl.BlockSpec(memory_space=pltpu.HBM)] * len(operands),
        out_specs=pl.BlockSpec(memory_space=vmem),
        scratch_shapes=[vmem(x.shape, x.dtype) for x in operands]
        + [
            vmem((devices, phases, rows, channels), F32),
            vmem((phases, devices, rows, channels), BF16),
            vmem((phases, devices, rows, channels), BF16),
            vmem((2, rows_count, cols_count // 2, key_blk, lanes), BF16),
            vmem((devices, rows, channels), F32),
            vmem((cols, tokens, channels), BF16),
            vmem((cols, channels, tokens), BF16),
            vmem((cols, tokens, channels), BF16),
            vmem((cols, tokens, channels), F32),
            vmem((2, cols_count // 2, lanes, tokens), F32),
            vmem((phases, devices, rows, channels), BF16),
            vmem((phases, devices, rows, channels), BF16),
            dma((len(operands),)),
        ]
        + [dma, dma((phases,))]
        + [dma] * 7
        + [dma((phases,))],
        compiler_params=pltpu.CompilerParams(
            collective_id=0, has_side_effects=True, vmem_limit_bytes=56 * 1024 * 1024
        ),
        cost_estimate=pl.CostEstimate(
            flops=2 * tokens * tokens * heads * channels * cols * 2,
            bytes_accessed=4 * slab.size,
            transcendentals=tokens * tokens * heads * cols,
        ),
        name="triangle",
    )(*operands)


def solution(mesh):
    placed = (P(("row", "col"), None, None), P("row", "col", None)) + (P(),) * 10
    return jax.shard_map(
        per_device,
        mesh=mesh,
        in_specs=placed,
        out_specs=P(("row", "col"), None, None),
        check_vma=False,
    )
```

```python
import functools
import math

import jax
import jax.numpy as jnp
from jax import lax
from jax.experimental import pallas as pl
from jax.experimental.pallas import tpu as pltpu
from jax.sharding import PartitionSpec as P

MESH = pl.DeviceIdType.MESH
F32 = jnp.float32
BF16 = jnp.bfloat16


def normalize(values, gain):
    center = jnp.mean(values, axis=-1, keepdims=True)
    moved = values - center
    spread = jnp.mean(jnp.square(moved), axis=-1, keepdims=True)
    return moved * lax.rsqrt(spread + 1e-05) * gain


def kernel(rows_count, cols_count, *refs):
    hbm, out_ref = refs[:12], refs[12]
    (
        slab_ref,
        pair_ref,
        mask_ref,
        gain_ref,
        wq_ref,
        wk_ref,
        wv_ref,
        wg_ref,
        gate_bias_ref,
        wb_ref,
        wo_ref,
        out_bias_ref,
    ) = local = refs[13:25]
    (
        slab_f32,
        slab_send,
        slab_recv,
        bias,
        chunk_f32,
        query,
        key_t,
        value,
        gate,
        bias_t,
        back_send,
        back_recv,
        in_sem,
        slab_ss,
        slab_rs,
        line_ss,
        line_rs,
        plane_ss,
        plane_rs,
        core_ss,
        core_rs,
        back_ss,
        back_rs,
    ) = refs[25:]
    devices = rows_count * cols_count
    tok, width, channels = slab_ref.shape
    key_blk, query_blk, _ = pair_ref.shape
    heads = wb_ref.shape[0]
    head_dim = channels // heads
    cols = width // devices
    tokens = devices * tok
    lanes = heads * query_blk
    owners = query_blk // tok
    scale = 1.0 / math.sqrt(head_dim)
    cores = 2
    line = cols_count // cores
    group = 2 - line % 2
    phases = 2 - cols % 2
    per = cols // phases
    my_row, my_col = lax.axis_index("row"), lax.axis_index("col")
    my_line, core = lax.div(my_col, cores), lax.rem(my_col, cores)
    me = my_row * cols_count + my_col

    def fetch(i):
        return pltpu.make_async_copy(hbm[i], local[i], in_sem.at[i])

    for i in (0, 3, 1, 9, 2, 4, 5, 6, 7, 8, 10, 11):
        fetch(i).start()

    def place(p):
        return (lax.div(p, cols_count), lax.rem(p, cols_count))

    def wait_bytes(ref, sem):
        pltpu.make_async_copy(ref, ref, sem).wait()

    def send(src, dst, send_sem, recv_sem, target):
        pltpu.make_async_remote_copy(
            src_ref=src,
            dst_ref=dst,
            send_sem=send_sem,
            recv_sem=recv_sem,
            device_id=target,
            device_id_type=MESH,
        ).start()

    barrier = pltpu.get_barrier_semaphore()

    def each_peer(act):
        def step(n, carry):
            r = lax.rem(my_row + n, rows_count)
            for m in range(cols_count):
                c = lax.rem(my_col + m, cols_count)
                if m:
                    act(r * cols_count + c, (r, c))
                else:

                    @pl.when(n > 0)
                    def _():
                        act(r * cols_count + c, (r, c))

            return carry

        lax.fori_loop(0, rows_count, step, 0)

    def greet(p, target):
        pl.semaphore_signal(barrier, inc=1, device_id=target, device_id_type=MESH)

    each_peer(greet)

    fetch(0).wait()
    fetch(3).wait()
    gain = gain_ref[...]
    flat = slab_f32.reshape(width * tok, channels)
    for t in range(tok):
        flat[t * width : (t + 1) * width, :] = normalize(slab_ref[t].astype(F32), gain)
    def cut_slab(f):
        for p in range(devices):
            starts = [p * cols + f * per + jj for jj in range(per)]
            parts = [flat[pl.ds(start, tok, stride=width), :] for start in starts]
            slab_send[f, p] = jnp.concatenate(parts, axis=0).astype(BF16)
        slab_recv[f, me] = slab_send[f, me]

    cut_slab(0)
    pl.semaphore_wait(barrier, devices - 1)

    def send_slab(f):
        def act(p, target):
            send(slab_send.at[f, p], slab_recv.at[f, me], slab_ss, slab_rs.at[f], target)

        each_peer(act)

    send_slab(0)

    fetch(1).wait()
    fetch(9).wait()
    lane_head = lax.broadcasted_iota(jnp.int32, (heads, lanes), 1) // query_blk
    spread_mat = (lane_head == lax.broadcasted_iota(jnp.int32, (heads, lanes), 0)).astype(F32)
    wide = lax.dot_general(
        wb_ref[...],
        spread_mat.astype(BF16),
        (((0,), (0,)), ((), ())),
        preferred_element_type=F32,
    ).astype(BF16)
    part, step_k = 4, 16
    lane_query = lax.rem(lax.broadcasted_iota(jnp.int32, (part, query_blk, lanes), 2), query_blk)
    own_query = lane_query == lax.broadcasted_iota(jnp.int32, (part, query_blk, lanes), 1)
    for k in range(0, key_blk, step_k):
        sums = []
        for kk in range(k, k + step_k, part):
            rows = pair_ref[kk : kk + part].astype(F32).reshape(part * query_blk, channels)
            normed = normalize(rows, gain).astype(BF16)
            spread = jnp.dot(normed, wide, preferred_element_type=F32)
            spread = jnp.where(own_query, spread.reshape(part, query_blk, lanes), 0.0)
            sums.append(jnp.sum(spread, axis=1))
        bias[core, my_row, my_line, k : k + step_k, :] = jnp.concatenate(sums, axis=0).astype(BF16)
    for n in range(1, line):
        z = lax.rem(my_line + n, line)
        tile = bias.at[core, my_row, my_line]
        send(tile, tile, line_ss, line_rs, (my_row, z * cores + core))

    for f in range(1, phases):
        cut_slab(f)
        send_slab(f)

    wait_bytes(bias.at[core, my_row, pl.ds(0, line - 1)], line_rs)
    block = bias.at[core, my_row]
    for n in range(1, rows_count):
        r = lax.rem(my_row + n, rows_count)
        send(block, block, plane_ss, plane_rs, (r, my_col))
    send(block, block, core_ss, core_rs, (my_row, my_col + 1 - 2 * core))

    for i in (2, 4, 5, 6, 7, 8, 10, 11):
        fetch(i).wait()
    joined_w = jnp.concatenate([wq_ref[...], wk_ref[...], wv_ref[...], wg_ref[...]], axis=1)

    def project(f):
        wait_bytes(slab_recv.at[f, pl.ds(0, devices - 1)], slab_rs.at[f])
        chunk_f32[...] = slab_recv[f].astype(F32)
        for j in range(per):
            jj = f * per + j
            rows = chunk_f32[:, j * tok : (j + 1) * tok, :].reshape(tokens, channels).astype(BF16)
            joined = jnp.dot(rows, joined_w, preferred_element_type=F32)
            query[jj] = joined[:, :channels].astype(BF16)
            key_t[jj] = joined[:, channels : 2 * channels].T.astype(BF16)
            value[jj] = joined[:, 2 * channels : 3 * channels].astype(BF16)
            gate[jj] = jax.nn.sigmoid(joined[:, 3 * channels :] + gate_bias_ref[...])

    project(0)

    wait_bytes(bias.at[core, pl.ds(0, rows_count - 1)], plane_rs)
    for n in range(1, rows_count):
        other = bias.at[core, lax.rem(my_row + n, rows_count)]
        send(other, other, core_ss, core_rs, (my_row, my_col + 1 - 2 * core))

    row_head = lax.broadcasted_iota(jnp.int32, (group * lanes, channels), 0) // query_blk
    chan_head = lax.broadcasted_iota(jnp.int32, (group * lanes, channels), 1) // head_dim
    own_head = lax.rem(row_head, heads) == chan_head
    shift = (mask_ref[...].astype(F32) - 1.0) * 1000000000.0

    def turn_bias(half):
        def step(z, carry):
            bias_t[half, z] = bias[half, :, z].astype(F32).reshape(tokens, lanes).T
            return carry

        lax.fori_loop(0, line, step, 0)

    def attend_blocks(f, half, z):
        at = [
            pl.multiple_of(((z + m) * cores + half) * query_blk, query_blk) for m in range(group)
        ]
        bias_rows = bias_t[half, pl.ds(z, group)].reshape(group * lanes, tokens)
        every = range(f * per, f * per + per)
        scores = []
        for jj in every:
            copies = []
            for m in range(group):
                copies += [query[jj, pl.ds(at[m], query_blk), :].astype(F32)] * heads
            q_heads = jnp.where(own_head, jnp.concatenate(copies, axis=0), 0.0).astype(BF16)
            scores.append(jnp.dot(q_heads, key_t[jj], preferred_element_type=F32))
        weights, denoms, numers = [], [], []
        for x, jj in zip(scores, every):
            tiles, sums = [], []
            for start in range(0, group * lanes, query_blk):
                own = slice(start, start + query_blk)
                tile = (x[own] * scale + bias_rows[own]) + shift
                tile = jnp.exp(tile - jnp.max(tile, axis=1, keepdims=True))
                sums.append(jnp.sum(tile, axis=1, keepdims=True))
                tiles.append(tile.astype(BF16))
            weights.append(jnp.concatenate(tiles, axis=0))
            denoms.append(jnp.concatenate(sums, axis=0))
        for x, jj in zip(weights, every):
            numers.append(jnp.dot(x, value[jj], preferred_element_type=F32))
        hidden = []
        for numer, denom, jj in zip(numers, denoms, every):
            spread = jnp.where(own_head, numer * (1.0 / denom), 0.0)
            for m in range(group):
                base = m * lanes
                attended = spread[base : base + query_blk]
                for h in range(1, heads):
                    start = base + h * query_blk
                    attended = attended + spread[start : start + query_blk]
                hidden.append((gate[jj, pl.ds(at[m], query_blk), :] * attended).astype(BF16))
        update = (
            jnp.dot(jnp.concatenate(hidden, axis=0), wo_ref[...], preferred_element_type=F32)
            + out_bias_ref[...]
        )
        for m in range(group):
            for o in range(owners):
                starts = [(j * group + m) * query_blk + o * tok for j in range(per)]
                back_send[f, ((z + m) * cores + half) * owners + o] = jnp.concatenate(
                    [update[start : start + tok] for start in starts], axis=0
                ).astype(BF16)

    def send_back(f, half, z):
        for o in range(owners):
            p = (z * cores + half) * owners + o

            @pl.when(p != me)
            def _():
                send(back_send.at[f, p], back_recv.at[f, me], back_ss, back_rs.at[f], place(p))

    def attend_half(f, half):
        firsts = [
            lax.rem(lax.div(my_line, group) + n, line // group) * group
            for n in range(line // group)
        ]
        width_z = 1
        for base in range(0, len(firsts), width_z):
            some = firsts[base : base + width_z]
            for first in some:
                attend_blocks(f, half, first)
            for first in some:
                for m in range(group):
                    send_back(f, half, first + m)

    turn_bias(core)
    attend_half(0, core)
    wait_bytes(bias.at[1 - core], core_rs)
    turn_bias(1 - core)
    attend_half(0, 1 - core)
    for f in range(1, phases):
        project(f)
        attend_half(f, core)
        attend_half(f, 1 - core)
    for f in range(phases):
        back_recv[f, me] = back_send[f, me]

    wait_bytes(slab_send.at[:, pl.ds(0, devices - 1)], slab_ss)
    wait_bytes(bias.at[core, my_row, pl.ds(0, line - 1)], line_ss)
    wait_bytes(bias.at[core, pl.ds(0, rows_count - 1)], plane_ss)
    wait_bytes(bias.at[core], core_ss)
    wait_bytes(back_send.at[:, pl.ds(0, devices - 1)], back_ss)
    for f in range(phases):
        wait_bytes(back_recv.at[f, pl.ds(0, devices - 1)], back_rs.at[f])
        slab_f32[:, f] = back_recv[f].astype(F32)
    for t in range(tok):
        out_ref[t] = flat[pl.ds(t, width, stride=tok), :].astype(BF16)


def per_device(
    slab, pair, mask, ln_gain, w_query, w_key, w_value, w_gate, gate_bias, w_bias, w_out, out_bias
):
    rows_count = lax.axis_size("row")
    cols_count = lax.axis_size("col")
    devices = rows_count * cols_count
    tok, width, channels = slab.shape
    key_blk, query_blk, _ = pair.shape
    heads = w_bias.shape[1]
    cols = width // devices
    tokens = devices * tok
    lanes = heads * query_blk
    phases = 2 - cols % 2
    rows = cols // phases * tok
    operands = (
        slab,
        pair,
        mask.reshape(1, -1),
        ln_gain.reshape(1, -1),
        w_query,
        w_key,
        w_value,
        w_gate,
        gate_bias.reshape(1, -1),
        w_bias.T,
        w_out,
        out_bias.reshape(1, -1),
    )
    dma = pltpu.SemaphoreType.DMA
    vmem = pltpu.VMEM
    return pl.pallas_call(
        functools.partial(kernel, rows_count, cols_count),
        out_shape=jax.ShapeDtypeStruct(slab.shape, BF16),
        in_specs=[pl.BlockSpec(memory_space=pltpu.HBM)] * len(operands),
        out_specs=pl.BlockSpec(memory_space=vmem),
        scratch_shapes=[vmem(x.shape, x.dtype) for x in operands]
        + [
            vmem((devices, phases, rows, channels), F32),
            vmem((phases, devices, rows, channels), BF16),
            vmem((phases, devices, rows, channels), BF16),
            vmem((2, rows_count, cols_count // 2, key_blk, lanes), BF16),
            vmem((devices, rows, channels), F32),
            vmem((cols, tokens, channels), BF16),
            vmem((cols, channels, tokens), BF16),
            vmem((cols, tokens, channels), BF16),
            vmem((cols, tokens, channels), F32),
            vmem((2, cols_count // 2, lanes, tokens), F32),
            vmem((phases, devices, rows, channels), BF16),
            vmem((phases, devices, rows, channels), BF16),
            dma((len(operands),)),
        ]
        + [dma, dma((phases,))]
        + [dma] * 7
        + [dma((phases,))],
        compiler_params=pltpu.CompilerParams(
            collective_id=0, has_side_effects=True, vmem_limit_bytes=56 * 1024 * 1024
        ),
        cost_estimate=pl.CostEstimate(
            flops=2 * tokens * tokens * heads * channels * cols * 2,
            bytes_accessed=4 * slab.size,
            transcendentals=tokens * tokens * heads * cols,
        ),
        name="triangle",
    )(*operands)


def solution(mesh):
    placed = (P(("row", "col"), None, None), P("row", "col", None)) + (P(),) * 10
    return jax.shard_map(
        per_device,
        mesh=mesh,
        in_specs=placed,
        out_specs=P(("row", "col"), None, None),
        check_vma=False,
    )
```

```python
import functools
import math

import jax
import jax.numpy as jnp
from jax import lax
from jax.experimental import pallas as pl
from jax.experimental.pallas import tpu as pltpu
from jax.sharding import PartitionSpec as P

MESH = pl.DeviceIdType.MESH
F32 = jnp.float32
BF16 = jnp.bfloat16


def normalize(values, gain):
    center = jnp.mean(values, axis=-1, keepdims=True)
    moved = values - center
    spread = jnp.mean(jnp.square(moved), axis=-1, keepdims=True)
    return moved * lax.rsqrt(spread + 1e-05) * gain


def kernel(rows_count, cols_count, *refs):
    hbm, out_ref = refs[:12], refs[12]
    (
        slab_ref,
        pair_ref,
        mask_ref,
        gain_ref,
        wq_ref,
        wk_ref,
        wv_ref,
        wg_ref,
        gate_bias_ref,
        wb_ref,
        wo_ref,
        out_bias_ref,
    ) = local = refs[13:25]
    (
        slab_f32,
        slab_send,
        slab_recv,
        bias,
        chunk_f32,
        query,
        key_t,
        value,
        gate,
        bias_t,
        back_send,
        back_recv,
        in_sem,
        slab_ss,
        slab_rs,
        line_ss,
        line_rs,
        plane_ss,
        plane_rs,
        core_ss,
        core_rs,
        back_ss,
        back_rs,
    ) = refs[25:]
    devices = rows_count * cols_count
    tok, width, channels = slab_ref.shape
    key_blk, query_blk, _ = pair_ref.shape
    heads = wb_ref.shape[0]
    head_dim = channels // heads
    cols = width // devices
    tokens = devices * tok
    lanes = heads * query_blk
    owners = query_blk // tok
    scale = 1.0 / math.sqrt(head_dim)
    cores = 2
    line = cols_count // cores
    group = 2 - line % 2
    phases = 2 - cols % 2
    per = cols // phases
    my_row, my_col = lax.axis_index("row"), lax.axis_index("col")
    my_line, core = lax.div(my_col, cores), lax.rem(my_col, cores)
    me = my_row * cols_count + my_col

    def fetch(i):
        return pltpu.make_async_copy(hbm[i], local[i], in_sem.at[i])

    for i in (0, 3, 1, 9, 2, 4, 5, 6, 7, 8, 10, 11):
        fetch(i).start()

    def place(p):
        return (lax.div(p, cols_count), lax.rem(p, cols_count))

    def wait_bytes(ref, sem):
        pltpu.make_async_copy(ref, ref, sem).wait()

    def send(src, dst, send_sem, recv_sem, target):
        pltpu.make_async_remote_copy(
            src_ref=src,
            dst_ref=dst,
            send_sem=send_sem,
            recv_sem=recv_sem,
            device_id=target,
            device_id_type=MESH,
        ).start()

    barrier = pltpu.get_barrier_semaphore()

    def each_peer(act):
        def step(n, carry):
            r = lax.rem(my_row + n, rows_count)
            for m in range(cols_count):
                c = lax.rem(my_col + m, cols_count)
                if m:
                    act(r * cols_count + c, (r, c))
                else:

                    @pl.when(n > 0)
                    def _():
                        act(r * cols_count + c, (r, c))

            return carry

        lax.fori_loop(0, rows_count, step, 0)

    def greet(p, target):
        pl.semaphore_signal(barrier, inc=1, device_id=target, device_id_type=MESH)

    each_peer(greet)

    fetch(0).wait()
    fetch(3).wait()
    gain = gain_ref[...]
    flat = slab_f32.reshape(width * tok, channels)
    for t in range(tok):
        flat[t * width : (t + 1) * width, :] = normalize(slab_ref[t].astype(F32), gain)
    def cut_slab(f):
        for p in range(devices):
            starts = [p * cols + f * per + jj for jj in range(per)]
            parts = [flat[pl.ds(start, tok, stride=width), :] for start in starts]
            slab_send[f, p] = jnp.concatenate(parts, axis=0).astype(BF16)
        slab_recv[f, me] = slab_send[f, me]

    cut_slab(0)
    pl.semaphore_wait(barrier, devices - 1)

    def send_slab(f):
        def act(p, target):
            send(slab_send.at[f, p], slab_recv.at[f, me], slab_ss, slab_rs.at[f], target)

        each_peer(act)

    send_slab(0)

    fetch(1).wait()
    fetch(9).wait()
    lane_head = lax.broadcasted_iota(jnp.int32, (heads, lanes), 1) // query_blk
    spread_mat = (lane_head == lax.broadcasted_iota(jnp.int32, (heads, lanes), 0)).astype(F32)
    wide = lax.dot_general(
        wb_ref[...],
        spread_mat.astype(BF16),
        (((0,), (0,)), ((), ())),
        preferred_element_type=F32,
    ).astype(BF16)
    part, step_k = 4, 16
    lane_query = lax.rem(lax.broadcasted_iota(jnp.int32, (part, query_blk, lanes), 2), query_blk)
    own_query = lane_query == lax.broadcasted_iota(jnp.int32, (part, query_blk, lanes), 1)
    for k in range(0, key_blk, step_k):
        sums = []
        for kk in range(k, k + step_k, part):
            rows = pair_ref[kk : kk + part].astype(F32).reshape(part * query_blk, channels)
            normed = normalize(rows, gain).astype(BF16)
            spread = jnp.dot(normed, wide, preferred_element_type=F32)
            spread = jnp.where(own_query, spread.reshape(part, query_blk, lanes), 0.0)
            sums.append(jnp.sum(spread, axis=1))
        bias[core, my_row, my_line, k : k + step_k, :] = jnp.concatenate(sums, axis=0).astype(BF16)
    for n in range(1, line):
        z = lax.rem(my_line + n, line)
        tile = bias.at[core, my_row, my_line]
        send(tile, tile, line_ss, line_rs, (my_row, z * cores + core))

    wait_bytes(bias.at[core, my_row, pl.ds(0, line - 1)], line_rs)
    block = bias.at[core, my_row]
    for n in range(1, rows_count):
        r = lax.rem(my_row + n, rows_count)
        send(block, block, plane_ss, plane_rs, (r, my_col))
    send(block, block, core_ss, core_rs, (my_row, my_col + 1 - 2 * core))

    for f in range(1, phases):
        cut_slab(f)
        send_slab(f)

    for i in (2, 4, 5, 6, 7, 8, 10, 11):
        fetch(i).wait()
    joined_w = jnp.concatenate([wq_ref[...], wk_ref[...], wv_ref[...], wg_ref[...]], axis=1)

    def project(f):
        wait_bytes(slab_recv.at[f, pl.ds(0, devices - 1)], slab_rs.at[f])
        chunk_f32[...] = slab_recv[f].astype(F32)
        for j in range(per):
            jj = f * per + j
            rows = chunk_f32[:, j * tok : (j + 1) * tok, :].reshape(tokens, channels).astype(BF16)
            joined = jnp.dot(rows, joined_w, preferred_element_type=F32)
            query[jj] = joined[:, :channels].astype(BF16)
            key_t[jj] = joined[:, channels : 2 * channels].T.astype(BF16)
            value[jj] = joined[:, 2 * channels : 3 * channels].astype(BF16)
            gate[jj] = jax.nn.sigmoid(joined[:, 3 * channels :] + gate_bias_ref[...])

    project(0)

    wait_bytes(bias.at[core, pl.ds(0, rows_count - 1)], plane_rs)
    for n in range(1, rows_count):
        other = bias.at[core, lax.rem(my_row + n, rows_count)]
        send(other, other, core_ss, core_rs, (my_row, my_col + 1 - 2 * core))

    row_head = lax.broadcasted_iota(jnp.int32, (group * lanes, channels), 0) // query_blk
    chan_head = lax.broadcasted_iota(jnp.int32, (group * lanes, channels), 1) // head_dim
    own_head = lax.rem(row_head, heads) == chan_head
    shift = (mask_ref[...].astype(F32) - 1.0) * 1000000000.0

    def turn_bias(half):
        def step(z, carry):
            bias_t[half, z] = bias[half, :, z].astype(F32).reshape(tokens, lanes).T
            return carry

        lax.fori_loop(0, line, step, 0)

    def attend_blocks(f, half, z):
        at = [
            pl.multiple_of(((z + m) * cores + half) * query_blk, query_blk) for m in range(group)
        ]
        bias_rows = bias_t[half, pl.ds(z, group)].reshape(group * lanes, tokens)
        every = range(f * per, f * per + per)
        scores = []
        for jj in every:
            copies = []
            for m in range(group):
                copies += [query[jj, pl.ds(at[m], query_blk), :].astype(F32)] * heads
            q_heads = jnp.where(own_head, jnp.concatenate(copies, axis=0), 0.0).astype(BF16)
            scores.append(jnp.dot(q_heads, key_t[jj], preferred_element_type=F32))
        weights, denoms, numers = [], [], []
        for x, jj in zip(scores, every):
            tiles, sums = [], []
            for start in range(0, group * lanes, query_blk):
                own = slice(start, start + query_blk)
                tile = (x[own] * scale + bias_rows[own]) + shift
                tile = jnp.exp(tile - jnp.max(tile, axis=1, keepdims=True))
                sums.append(jnp.sum(tile, axis=1, keepdims=True))
                tiles.append(tile.astype(BF16))
            weights.append(jnp.concatenate(tiles, axis=0))
            denoms.append(jnp.concatenate(sums, axis=0))
        for x, jj in zip(weights, every):
            numers.append(jnp.dot(x, value[jj], preferred_element_type=F32))
        hidden = []
        for numer, denom, jj in zip(numers, denoms, every):
            spread = jnp.where(own_head, numer * (1.0 / denom), 0.0)
            for m in range(group):
                base = m * lanes
                attended = spread[base : base + query_blk]
                for h in range(1, heads):
                    start = base + h * query_blk
                    attended = attended + spread[start : start + query_blk]
                hidden.append((gate[jj, pl.ds(at[m], query_blk), :] * attended).astype(BF16))
        update = (
            jnp.dot(jnp.concatenate(hidden, axis=0), wo_ref[...], preferred_element_type=F32)
            + out_bias_ref[...]
        )
        for m in range(group):
            for o in range(owners):
                starts = [(j * group + m) * query_blk + o * tok for j in range(per)]
                back_send[f, ((z + m) * cores + half) * owners + o] = jnp.concatenate(
                    [update[start : start + tok] for start in starts], axis=0
                ).astype(BF16)

    def send_back(f, half, z):
        for o in range(owners):
            p = (z * cores + half) * owners + o

            @pl.when(p != me)
            def _():
                send(back_send.at[f, p], back_recv.at[f, me], back_ss, back_rs.at[f], place(p))

    def attend_half(f, half):
        firsts = [
            lax.rem(lax.div(my_line, group) + n, line // group) * group
            for n in range(line // group)
        ]
        width_z = 1
        for base in range(0, len(firsts), width_z):
            some = firsts[base : base + width_z]
            for first in some:
                attend_blocks(f, half, first)
            for first in some:
                for m in range(group):
                    send_back(f, half, first + m)

    turn_bias(core)
    attend_half(0, core)
    wait_bytes(bias.at[1 - core], core_rs)
    turn_bias(1 - core)
    attend_half(0, 1 - core)
    for f in range(1, phases):
        project(f)
        attend_half(f, core)
        attend_half(f, 1 - core)
    for f in range(phases):
        back_recv[f, me] = back_send[f, me]

    wait_bytes(slab_send.at[:, pl.ds(0, devices - 1)], slab_ss)
    wait_bytes(bias.at[core, my_row, pl.ds(0, line - 1)], line_ss)
    wait_bytes(bias.at[core, pl.ds(0, rows_count - 1)], plane_ss)
    wait_bytes(bias.at[core], core_ss)
    wait_bytes(back_send.at[:, pl.ds(0, devices - 1)], back_ss)
    for f in range(phases):
        wait_bytes(back_recv.at[f, pl.ds(0, devices - 1)], back_rs.at[f])
        slab_f32[:, f] = back_recv[f].astype(F32)
    for t in range(tok):
        out_ref[t] = flat[pl.ds(t, width, stride=tok), :].astype(BF16)


def per_device(
    slab, pair, mask, ln_gain, w_query, w_key, w_value, w_gate, gate_bias, w_bias, w_out, out_bias
):
    rows_count = lax.axis_size("row")
    cols_count = lax.axis_size("col")
    devices = rows_count * cols_count
    tok, width, channels = slab.shape
    key_blk, query_blk, _ = pair.shape
    heads = w_bias.shape[1]
    cols = width // devices
    tokens = devices * tok
    lanes = heads * query_blk
    phases = 2 - cols % 2
    rows = cols // phases * tok
    operands = (
        slab,
        pair,
        mask.reshape(1, -1),
        ln_gain.reshape(1, -1),
        w_query,
        w_key,
        w_value,
        w_gate,
        gate_bias.reshape(1, -1),
        w_bias.T,
        w_out,
        out_bias.reshape(1, -1),
    )
    dma = pltpu.SemaphoreType.DMA
    vmem = pltpu.VMEM
    return pl.pallas_call(
        functools.partial(kernel, rows_count, cols_count),
        out_shape=jax.ShapeDtypeStruct(slab.shape, BF16),
        in_specs=[pl.BlockSpec(memory_space=pltpu.HBM)] * len(operands),
        out_specs=pl.BlockSpec(memory_space=vmem),
        scratch_shapes=[vmem(x.shape, x.dtype) for x in operands]
        + [
            vmem((devices, phases, rows, channels), F32),
            vmem((phases, devices, rows, channels), BF16),
            vmem((phases, devices, rows, channels), BF16),
            vmem((2, rows_count, cols_count // 2, key_blk, lanes), BF16),
            vmem((devices, rows, channels), F32),
            vmem((cols, tokens, channels), BF16),
            vmem((cols, channels, tokens), BF16),
            vmem((cols, tokens, channels), BF16),
            vmem((cols, tokens, channels), F32),
            vmem((2, cols_count // 2, lanes, tokens), F32),
            vmem((phases, devices, rows, channels), BF16),
            vmem((phases, devices, rows, channels), BF16),
            dma((len(operands),)),
        ]
        + [dma, dma((phases,))]
        + [dma] * 7
        + [dma((phases,))],
        compiler_params=pltpu.CompilerParams(
            collective_id=0, has_side_effects=True, vmem_limit_bytes=56 * 1024 * 1024
        ),
        cost_estimate=pl.CostEstimate(
            flops=2 * tokens * tokens * heads * channels * cols * 2,
            bytes_accessed=4 * slab.size,
            transcendentals=tokens * tokens * heads * cols,
        ),
        name="triangle",
    )(*operands)


def solution(mesh):
    placed = (P(("row", "col"), None, None), P("row", "col", None)) + (P(),) * 10
    return jax.shard_map(
        per_device,
        mesh=mesh,
        in_specs=placed,
        out_specs=P(("row", "col"), None, None),
        check_vma=False,
    )
```
